32 devices in a mesh: half: 2 (over x), dp: 16 (over z, y, core).
Axes of the slice: x: 2, y: 2, z: 4, core: 2. Of those that a mesh axis runs over, the one named last changes fastest.
Arguments:
- frames: bfloat16 [32768, 1024], P(('half', 'dp')), may hold values from -6 to 6
- skip_rows: bfloat16 [32768, 1024], P(('half', 'dp')), may hold values from -6 to 6
- lengths: int32 [32, 4], P(('half', 'dp')), may hold values from 1 to 640, 1024 in all within a row
- merge_weight: bfloat16 [2048, 1024], replicated, may hold values from -0.125 to 0.125
- merge_bias: float32 [1024], replicated, may hold values from -3 to 3
- norm1_gain: float32 [1024], replicated, may hold values from 0.1 to 1.9
- norm1_bias: float32 [1024], replicated, may hold values from -1.75 to 1.75
- qkv_weight: bfloat16 [1024, 3072], replicated, may hold values from -0.1875 to 0.1875
- out_weight: bfloat16 [1024, 1024], replicated, may hold values from -0.5 to 0.5
- norm2_gain: float32 [1024], replicated, may hold values from 0.1 to 1.9
- norm2_bias: float32 [1024], replicated, may hold values from -1.75 to 1.75
- up_weight: bfloat16 [1024, 4096], replicated, may hold values from -0.1875 to 0.1875
- up_bias: float32 [4096], replicated, may hold values from -3 to 3
- down_weight: bfloat16 [4096, 1024], replicated, may hold values from -0.09375 to 0.09375
- down_bias: float32 [1024], replicated, may hold values from -3 to 3
- cotangent: bfloat16 [32768, 1024], P(('half', 'dp')), may hold values from -12 to 12
Outputs:
- output: bfloat16 [32768, 1024], P(('half', 'dp'))
- frames_grad: bfloat16 [32768, 1024], P(('half', 'dp'))
- skip_grad: bfloat16 [32768, 1024], P(('half', 'dp'))
- merge_weight_grad: float32 [2048, 1024], P(('half', 'dp'))
- merge_bias_grad: float32 [1024], P(('half', 'dp'))
- norm1_gain_grad: float32 [1024], P(('half', 'dp'))
- norm1_bias_grad: float32 [1024], P(('half', 'dp'))
- qkv_weight_grad: float32 [1024, 3072], P(('half', 'dp'))
- out_weight_grad: float32 [1024, 1024], P(('half', 'dp'))
- norm2_gain_grad: float32 [1024], P(('half', 'dp'))
- norm2_bias_grad: float32 [1024], P(('half', 'dp'))
- up_weight_grad: float32 [1024, 4096], P(('half', 'dp'))
- up_bias_grad: float32 [4096], P(('half', 'dp'))
- down_weight_grad: float32 [4096, 1024], P(('half', 'dp'))
- down_bias_grad: float32 [1024], P(('half', 'dp'))
The draws below stay inside these ranges and needn't reach their ends.
Inputs may be any that keep to these rules, and one draw needn't show every extreme that they name: Each row of lengths sums to 1024; its utterances fill the row in order.
All inputs are finite; a program needn't handle non-finite values.
Results may differ from the reference program's by a relative error of at most 0.014.
Values may be sent and summed in bfloat16 or wider, within the bound.
No kernel may reach another device: no remote copies, remote signals or barrier semaphores. Data moves between devices by JAX's collectives and lax.ppermute only.
A program may use at most 384 MiB of HBM per device.

```python
import math
import jax
import jax.numpy as jnp
import numpy as np
from jax import lax

D = 1024
H = 16
HD = 64
FF = 4096
ROW_LEN = 1024
UTT_ROW = 4
UTT_MOST = 640
ROWS = 32
TOKENS = 32768


def raised(values, own_key, source, target, parts, factor):
    owner, partner = [(jnp.arange(values.shape[axis_at]) // (values.shape[axis_at] // parts)).reshape([-1 if axis == axis_at else 1 for axis in range(values.ndim)]) for axis_at in (source, target)]
    chosen = jax.random.permutation(own_key, parts)[partner]
    strong = (owner == chosen) | (owner == (partner + parts // 2) % parts)
    return jnp.where(strong, factor * values, values)


def shard_levels(key, shape, split, low, high):
    gain = 1.0
    for dim, parts in split:
        draws = jax.random.uniform(jax.random.fold_in(jax.random.fold_in(key, 6), dim), (parts,), jnp.float32, low / len(split), high / len(split))
        gain = gain * jnp.repeat(jnp.exp(draws), shape[dim] // parts).reshape((-1,) + (1,) * (len(shape) - 1 - dim))
    return gain


def length_profile(count, total, most, slope):
    loads = [(1 << 20) // math.isqrt(standing ** slope) + 1 for standing in range(2, count + 1)]
    rest, holding = total - most - (count - 1), [1] * (count - 1)
    while rest > 0:
        free = [i for i in range(count - 1) if holding[i] < most]
        mass, left = sum([loads[i] for i in free]), rest
        for i in free:
            extra = min(most - holding[i], max(1, left * loads[i] // mass), rest)
            holding[i] = holding[i] + extra
            rest = rest - extra
    return np.array([most] + holding)


def ragged(own_key, amount, total, limit, skew):
    if amount == 2:
        one = jax.random.randint(own_key, (), max(1, total - limit), min(limit, total - 1) + 1)
        return jnp.stack([one, total - one])
    tallies = jnp.asarray(length_profile(amount, total, limit, skew), jnp.int32)
    couples = (amount - 1) // 2
    donor, receiver = tallies[1:1 + 2 * couples:2], tallies[2:2 + 2 * couples:2]
    slack = jnp.minimum(donor - 1, limit - receiver)
    shifted = jax.random.randint(jax.random.fold_in(own_key, 1), (couples,), 0, 1 << 20) % (slack + 1)
    tallies = tallies.at[1:1 + 2 * couples:2].set(donor - shifted).at[2:2 + 2 * couples:2].set(receiver + shifted)
    return tallies[jax.random.permutation(jax.random.fold_in(own_key, 2), amount)]


def noise(own_key, shape, spread, reach, shards=(), kind=jnp.bfloat16):
    values = spread * jax.random.normal(own_key, shape, jnp.float32)
    if shards:
        values = values * shard_levels(own_key, shape, shards, -0.22, 0.18)
    return jnp.clip(values, -reach, reach).astype(kind)


def heavy_noise(own_key, dims, scale, reach, cuts, heavy, kind=jnp.bfloat16):
    result = scale * jax.random.normal(own_key, dims, jnp.float32)
    if cuts:
        result = result * shard_levels(own_key, dims, cuts, -0.22, 0.18)
    return jnp.clip(raised(result, jax.random.fold_in(own_key, 3), *heavy), -reach, reach).astype(kind)


def setup_inputs(seed: int = 0) -> dict:
    seeds = jax.random.split(jax.random.key(seed), 17)
    frames = noise(seeds[0], (TOKENS, D), 1.0, 6.0, ((0, 32),))
    skip_rows = noise(seeds[1], (TOKENS, D), 1.0, 6.0, ((0, 32),))
    lengths = jax.vmap(lambda own: ragged(own, UTT_ROW, ROW_LEN, UTT_MOST, 2))(jax.random.split(seeds[2], ROWS)).reshape((ROWS, UTT_ROW)).astype(jnp.int32)
    merge_weight = noise(seeds[3], (2 * D, D), (2 * D) ** -0.5, 0.125)
    merge_bias = noise(seeds[4], (D,), 0.5, 3.0, (), jnp.float32)
    norm1_gain = jnp.clip(1.0 + 0.18 * jax.random.normal(seeds[5], (D,), jnp.float32), 0.1, 1.9)
    norm1_bias = noise(seeds[6], (D,), 0.3, 1.75, (), jnp.float32)
    qkv_weight = noise(seeds[7], (D, 3 * D), D ** -0.5, 0.1875)
    out_weight = noise(seeds[8], (D, D), (D // 8) ** -0.5, 0.5)
    norm2_gain = jnp.clip(1.0 + 0.18 * jax.random.normal(seeds[9], (D,), jnp.float32), 0.1, 1.9)
    norm2_bias = noise(seeds[10], (D,), 0.3, 1.75, (), jnp.float32)
    up_weight = noise(seeds[11], (D, FF), D ** -0.5, 0.1875)
    up_bias = noise(seeds[12], (FF,), 0.5, 3.0, (), jnp.float32)
    down_weight = noise(seeds[13], (FF, D), FF ** -0.5, 0.09375)
    down_bias = noise(seeds[14], (D,), 0.5, 3.0, (), jnp.float32)
    cotangent = heavy_noise(seeds[15], (TOKENS, D), 1.0, 12.0, ((0, 32),), (0, 1, 32, 2.75))
    return {"frames": frames, "skip_rows": skip_rows, "lengths": lengths, "merge_weight": merge_weight, "merge_bias": merge_bias, "norm1_gain": norm1_gain, "norm1_bias": norm1_bias, "qkv_weight": qkv_weight, "out_weight": out_weight, "norm2_gain": norm2_gain, "norm2_bias": norm2_bias, "up_weight": up_weight, "up_bias": up_bias, "down_weight": down_weight, "down_bias": down_bias, "cotangent": cotangent}


HIGHEST = lax.Precision.HIGHEST
epsilon = 1e-05
masked_score = -1000000000.0

@jax.custom_vjp
def low(v):
    return lax.optimization_barrier(v.astype(jnp.bfloat16)).astype(jnp.float32)

@jax.custom_vjp
def low_back(v):
    return v

def low_keep(v):
    return (low(v), None)

def low_pass(kept, grad):
    return (grad,)

def back_keep(v):
    return (v, None)

def back_low(kept, grad):
    return (low(grad),)
low.defvjp(low_keep, low_pass)
low_back.defvjp(back_keep, back_low)

def matmul_high(left_side, right_side):
    return jnp.dot(left_side, right_side, precision=HIGHEST, preferred_element_type=jnp.float32)

def norm_rows(values_in, gain_vector, shift_vector):
    row_mean = lax.optimization_barrier(jnp.mean(values_in, axis=-1, keepdims=True))
    centred = values_in - row_mean
    row_var = lax.optimization_barrier(jnp.mean(centred * centred, axis=-1, keepdims=True))
    return centred * lax.rsqrt(row_var + epsilon) * gain_vector + shift_vector

def exact_gelu(values_in):
    return jax.nn.gelu(values_in, approximate=False)

def head_slopes():
    return jnp.exp2(-8.0 * (jnp.arange(H, dtype=jnp.float32) + 1.0) / H)

def row_segments(length_row):
    length_ends = jnp.cumsum(length_row)
    position = jnp.arange(ROW_LEN, dtype=jnp.int32)
    return lax.optimization_barrier(jnp.sum((position[:, None] >= length_ends[None, :]).astype(jnp.int32), axis=1))

def layer_row(frame_row, skip_row, segment, weight_set):
    merge_weight, merge_bias, norm1_gain, norm1_bias, qkv_weight, out_weight, norm2_gain, norm2_bias, up_weight, up_bias, down_weight, down_bias = weight_set
    joined = jnp.concatenate([frame_row, skip_row], axis=1)
    hidden = low_back(matmul_high(joined, merge_weight) + merge_bias)
    normed = low(norm_rows(hidden, norm1_gain, norm1_bias))
    projected = low_back(low(matmul_high(normed, qkv_weight))).reshape(ROW_LEN, 3, H, HD)
    query_row = projected[:, 0]
    key_row = projected[:, 1]
    value_row = projected[:, 2]
    position = jnp.arange(ROW_LEN, dtype=jnp.int32)
    distance = jnp.abs(position[:, None] - position[None, :]).astype(jnp.float32)
    raw_scores = jnp.einsum('qhd,khd->hqk', query_row, key_row, precision=HIGHEST) * HD ** (-0.5)
    raw_scores = low_back(raw_scores - head_slopes()[:, None, None] * distance[None])
    same_segment = segment[:, None] == segment[None, :]
    masked = jnp.where(same_segment[None], raw_scores, masked_score)
    soft_weights = low(jax.nn.softmax(masked, axis=-1))
    mixed_heads = jnp.einsum('hqk,khd->qhd', soft_weights, value_row, precision=HIGHEST)
    mixed_heads = low_back(low(mixed_heads)).reshape(ROW_LEN, D)
    attention = low_back(matmul_high(mixed_heads, out_weight))
    residual = hidden + attention
    normed_two = low(norm_rows(residual, norm2_gain, norm2_bias))
    up_value = low_back(matmul_high(normed_two, up_weight) + up_bias)
    activated = low(exact_gelu(up_value))
    return residual + matmul_high(activated, down_weight) + down_bias

def reference(frames, skip_rows, lengths, merge_weight, merge_bias, norm1_gain, norm1_bias, qkv_weight, out_weight, norm2_gain, norm2_bias, up_weight, up_bias, down_weight, down_bias, cotangent):
    row_total = frames.shape[0] // ROW_LEN
    weight_set = tuple((member.astype(jnp.float32) for member in (merge_weight, merge_bias, norm1_gain, norm1_bias, qkv_weight, out_weight, norm2_gain, norm2_bias, up_weight, up_bias, down_weight, down_bias)))
    frame_rows = frames.astype(jnp.float32).reshape(row_total, ROW_LEN, D)
    mirror_rows = jnp.roll(skip_rows.astype(jnp.float32).reshape(row_total, ROW_LEN, D), row_total // 2, axis=0)
    cot_rows = cotangent.astype(jnp.float32).reshape(row_total, ROW_LEN, D)
    initial = jax.tree.map(jnp.zeros_like, weight_set)

    def row_step(running, row_item):
        frame_row, skip_row, length_row, cot_row = row_item
        segment = row_segments(length_row)

        def forward(frame_in, skip_in, weights_in):
            return layer_row(frame_in, skip_in, segment, weights_in)
        out_row, pullback = jax.vjp(forward, frame_row, skip_row, weight_set)
        frame_grad, skip_part, weight_grads = pullback(cot_row)
        running = jax.tree.map(jnp.add, running, weight_grads)
        return (running, (out_row.astype(jnp.bfloat16), frame_grad.astype(jnp.bfloat16), skip_part.astype(jnp.bfloat16)))
    gradients, (out_rows, frame_grads, skip_parts) = lax.scan(row_step, initial, (frame_rows, mirror_rows, lengths, cot_rows))
    skip_grad = jnp.roll(skip_parts, row_total // 2, axis=0).reshape(frames.shape[0], D)
    return (out_rows.reshape(frames.shape[0], D), frame_grads.reshape(frames.shape[0], D), skip_grad, gradients[0], gradients[1], gradients[2], gradients[3], gradients[4], gradients[5], gradients[6], gradients[7], gradients[8], gradients[9], gradients[10], gradients[11])
```

```python
import jax
import jax.numpy as jnp
from jax import lax
from jax.sharding import PartitionSpec as P

D = 1024
H = 16
HD = 64
ROW_LEN = 1024


epsilon = 1e-05
masked_score = -1000000000.0


def swapped(value, axis, apart):
    mask = 2**apart
    pairs = [(source, source ^ mask) for source in range(lax.axis_size(axis))]
    return lax.ppermute(value, axis, pairs)


def norm_rows(values_in, gain_vector, shift_vector):
    row_mean = jnp.mean(values_in, axis=-1, keepdims=True)
    centred = values_in - row_mean
    row_var = jnp.mean(centred * centred, axis=-1, keepdims=True)
    return centred * lax.rsqrt(row_var + epsilon) * gain_vector + shift_vector


def exact_gelu(values_in):
    return jax.nn.gelu(values_in, approximate=False)


def head_slopes():
    return jnp.exp2(-8.0 * (jnp.arange(H, dtype=jnp.float32) + 1.0) / H)


def row_segments(length_row):
    length_ends = jnp.cumsum(length_row)
    position = jnp.arange(ROW_LEN, dtype=jnp.int32)
    return jnp.sum((position[:, None] >= length_ends[None, :]).astype(jnp.int32), axis=1)


def contract_rows(left_side, right_side):
    return lax.dot_general(
        left_side, right_side, (((0,), (0,)), ((), ())), preferred_element_type=jnp.float32
    )


def contract_cols(left_side, right_side):
    return lax.dot_general(
        left_side, right_side, (((1,), (1,)), ((), ())), preferred_element_type=jnp.float32
    )


def score_block(query_block, key_row, block_start, segment, slopes, block_rows):
    raw_scores = jnp.einsum(
        "qhd,khd->hqk", query_block, key_row, preferred_element_type=jnp.float32
    ) * HD ** (-0.5)
    query_pos = block_start + jnp.arange(block_rows, dtype=jnp.int32)
    key_pos = jnp.arange(ROW_LEN, dtype=jnp.int32)
    distance = jnp.abs(query_pos[:, None] - key_pos[None, :]).astype(jnp.float32)
    raw_scores = raw_scores - slopes[:, None, None] * distance[None]
    query_segment = lax.dynamic_slice_in_dim(segment, block_start, block_rows)
    same_segment = query_segment[:, None] == segment[None, :]
    return jnp.where(same_segment[None], raw_scores, masked_score)


def attend_row(query_row, key_row, value_row, segment, slopes):
    block_rows = min(512, ROW_LEN)
    block_starts = jnp.arange(ROW_LEN // block_rows, dtype=jnp.int32) * block_rows

    def one_block(block_start):
        query_block = lax.dynamic_slice_in_dim(query_row, block_start, block_rows)
        scores = score_block(query_block, key_row, block_start, segment, slopes, block_rows)
        row_max = jnp.max(scores, axis=-1, keepdims=True)
        exponent = jnp.exp(scores - row_max)
        row_total = jnp.sum(exponent, axis=-1, keepdims=True)
        soft_low = (exponent / row_total).astype(jnp.bfloat16)
        mixed_block = jnp.einsum(
            "hqk,khd->qhd", soft_low, value_row, preferred_element_type=jnp.float32
        )
        return (mixed_block.astype(jnp.bfloat16), (row_max + jnp.log(row_total))[:, :, 0])

    mixed_blocks, log_blocks = lax.map(one_block, block_starts)
    return (mixed_blocks.reshape(ROW_LEN, H, HD), log_blocks)


def attend_row_back(query_row, key_row, value_row, grad_row, log_row, segment, slopes):
    block_rows = min(512, ROW_LEN)
    block_starts = jnp.arange(ROW_LEN // block_rows, dtype=jnp.int32) * block_rows

    def one_block(running, block_inputs):
        key_grad, value_grad = running
        block_start, log_block = block_inputs
        query_block = lax.dynamic_slice_in_dim(query_row, block_start, block_rows)
        grad_block = lax.dynamic_slice_in_dim(grad_row, block_start, block_rows)
        scores = score_block(query_block, key_row, block_start, segment, slopes, block_rows)
        soft_weights = jnp.exp(scores - log_block[:, :, None])
        soft_low = soft_weights.astype(jnp.bfloat16)
        value_grad = value_grad + jnp.einsum(
            "hqk,qhd->khd", soft_low, grad_block, preferred_element_type=jnp.float32
        )
        soft_grad = jnp.einsum(
            "qhd,khd->hqk", grad_block, value_row, preferred_element_type=jnp.float32
        )
        inner_sum = jnp.sum(soft_weights * soft_grad, axis=-1, keepdims=True)
        score_grad = (soft_weights * (soft_grad - inner_sum)).astype(jnp.bfloat16)
        query_grad = jnp.einsum(
            "hqk,khd->qhd", score_grad, key_row, preferred_element_type=jnp.float32
        ) * HD ** (-0.5)
        key_grad = key_grad + jnp.einsum(
            "hqk,qhd->khd", score_grad, query_block, preferred_element_type=jnp.float32
        ) * HD ** (-0.5)
        return ((key_grad, value_grad), query_grad)

    initial = jnp.zeros((ROW_LEN, H, HD), jnp.float32)
    (key_grad, value_grad), query_grad = lax.scan(
        one_block, (initial, initial), (block_starts, log_row)
    )
    return (query_grad.reshape(ROW_LEN, H, HD), key_grad, value_grad)


def mesh_bits():
    dp_bits = lax.axis_size("dp").bit_length() - 1
    half_bits = lax.axis_size("half").bit_length() - 1
    return [("half", bit) for bit in reversed(range(half_bits))] + [
        ("dp", bit) for bit in reversed(range(dp_bits))
    ]


def halve(block, order, kept_type):
    bits = mesh_bits()
    left = list(range(len(bits)))
    for step, digit in enumerate(order):
        axis, apart = bits[digit]
        mine = (lax.axis_index(axis) >> apart) & 1
        at = left.index(digit)
        left.pop(at)
        sent = lax.dynamic_index_in_dim(block, 1 - mine, at, keepdims=False)
        kept = lax.dynamic_index_in_dim(block, mine, at, keepdims=False)
        got = swapped(sent, axis, apart)
        block = kept.astype(jnp.float32) + got.astype(jnp.float32)
        if step < len(order) - 1:
            block = block.astype(kept_type)
    return block


def reduce_orders():
    count = len(mesh_bits())
    core, second = count - 1, count - 2
    rest = list(range(second - 1, 0, -1))
    return ([core, 0, second] + rest, [core, second, 0] + rest)


def sum_matrices(matrices):
    count = len(mesh_bits())
    results = []
    for matrix in matrices:
        rows, columns = matrix.shape
        block = matrix.astype(jnp.bfloat16).reshape((2,) * count + (rows >> count, columns))
        cut = columns // 2
        orders = reduce_orders()
        results.append(
            jnp.concatenate(
                [
                    halve(block[..., :cut], orders[0], jnp.bfloat16),
                    halve(block[..., cut:], orders[1], jnp.bfloat16),
                ],
                axis=1,
            )
        )
    return results


def sum_vectors(vectors):
    count = len(mesh_bits())
    parts = [vector.reshape(1 << count, -1) for vector in vectors]
    joined = jnp.concatenate(parts, axis=1)
    total = halve(joined.reshape((2,) * count + (joined.shape[1],)), reduce_orders()[0], jnp.float32)
    cuts = []
    start = 0
    for part in parts:
        cuts.append(total[start : start + part.shape[1]])
        start += part.shape[1]
    return cuts


def on_device(
    frames,
    skip_rows,
    lengths,
    merge_weight,
    merge_bias,
    norm1_gain,
    norm1_bias,
    qkv_weight,
    out_weight,
    norm2_gain,
    norm2_bias,
    up_weight,
    up_bias,
    down_weight,
    down_bias,
    cotangent,
):
    token_count = frames.shape[0]
    row_count = token_count // ROW_LEN
    slopes = head_slopes()
    segments = jax.vmap(row_segments)(lengths)
    mirror = swapped(skip_rows, "half", 0)
    joined = jnp.concatenate([frames, mirror], axis=1)
    hidden = jnp.dot(joined, merge_weight, preferred_element_type=jnp.float32) + merge_bias
    normed, norm_back_one = jax.vjp(norm_rows, hidden, norm1_gain, norm1_bias)
    normed_low = normed.astype(jnp.bfloat16)
    projected = jnp.dot(normed_low, qkv_weight, preferred_element_type=jnp.float32).astype(
        jnp.bfloat16
    )
    head_view = projected.reshape(row_count, ROW_LEN, 3, H, HD)
    query_rows = head_view[:, :, 0]
    key_rows = head_view[:, :, 1]
    value_rows = head_view[:, :, 2]

    def forward_row(row_inputs):
        query_row, key_row, value_row, segment = row_inputs
        return attend_row(query_row, key_row, value_row, segment, slopes)

    mixed_rows, log_rows = lax.map(forward_row, (query_rows, key_rows, value_rows, segments))
    mixed_heads = mixed_rows.reshape(token_count, D)
    attention = jnp.dot(mixed_heads, out_weight, preferred_element_type=jnp.float32)
    residual = hidden + attention
    normed_two, norm_back_two = jax.vjp(norm_rows, residual, norm2_gain, norm2_bias)
    normed_two_low = normed_two.astype(jnp.bfloat16)
    up_value = jnp.dot(normed_two_low, up_weight, preferred_element_type=jnp.float32) + up_bias
    activated, gelu_back = jax.vjp(exact_gelu, up_value)
    activated_low = activated.astype(jnp.bfloat16)
    output = (
        residual
        + jnp.dot(activated_low, down_weight, preferred_element_type=jnp.float32)
        + down_bias
    ).astype(jnp.bfloat16)
    grad_out = cotangent.astype(jnp.float32)
    down_weight_grad = contract_rows(activated_low, cotangent)
    down_bias_grad = jnp.sum(grad_out, axis=0)
    activated_grad = contract_cols(cotangent, down_weight)
    up_grad = gelu_back(activated_grad)[0].astype(jnp.bfloat16)
    up_bias_grad = jnp.sum(up_grad.astype(jnp.float32), axis=0)
    up_weight_grad = contract_rows(normed_two_low, up_grad)
    normed_two_grad = contract_cols(up_grad, up_weight)
    residual_part, gain_two_grad, shift_two_grad = norm_back_two(normed_two_grad)
    residual_grad = grad_out + residual_part
    attention_grad = residual_grad.astype(jnp.bfloat16)
    out_weight_grad = contract_rows(mixed_heads, attention_grad)
    mixed_grad = (
        contract_cols(attention_grad, out_weight)
        .astype(jnp.bfloat16)
        .reshape(row_count, ROW_LEN, H, HD)
    )

    def backward_row(row_inputs):
        query_row, key_row, value_row, grad_row, log_row, segment = row_inputs
        return attend_row_back(query_row, key_row, value_row, grad_row, log_row, segment, slopes)

    query_grads, key_grads, value_grads = lax.map(
        backward_row, (query_rows, key_rows, value_rows, mixed_grad, log_rows, segments)
    )
    projected_grad = (
        jnp.stack([query_grads, key_grads, value_grads], axis=2)
        .reshape(token_count, 3 * D)
        .astype(jnp.bfloat16)
    )
    qkv_weight_grad = contract_rows(normed_low, projected_grad)
    normed_grad = contract_cols(projected_grad, qkv_weight)
    hidden_part, gain_one_grad, shift_one_grad = norm_back_one(normed_grad)
    hidden_grad = (residual_grad + hidden_part).astype(jnp.bfloat16)
    merge_bias_grad = jnp.sum(hidden_grad.astype(jnp.float32), axis=0)
    merge_weight_grad = contract_rows(joined, hidden_grad)
    joined_grad = contract_cols(hidden_grad, merge_weight)
    frames_grad = joined_grad[:, :D].astype(jnp.bfloat16)
    skip_grad = swapped(joined_grad[:, D:].astype(jnp.bfloat16), "half", 0)
    matrices = sum_matrices(
        (merge_weight_grad, qkv_weight_grad, out_weight_grad, up_weight_grad, down_weight_grad)
    )
    vectors = sum_vectors(
        (
            merge_bias_grad,
            gain_one_grad,
            shift_one_grad,
            gain_two_grad,
            shift_two_grad,
            up_bias_grad,
            down_bias_grad,
        )
    )
    summed = (
        matrices[0],
        vectors[0],
        vectors[1],
        vectors[2],
        matrices[1],
        matrices[2],
        vectors[3],
        vectors[4],
        matrices[3],
        vectors[5],
        matrices[4],
        vectors[6],
    )
    return (
        output,
        frames_grad,
        skip_grad,
        summed[0],
        summed[1],
        summed[2],
        summed[3],
        summed[4],
        summed[5],
        summed[6],
        summed[7],
        summed[8],
        summed[9],
        summed[10],
        summed[11],
    )


def solution(mesh):
    in_specs = (
        P(("half", "dp"), None),
        P(("half", "dp"), None),
        P(("half", "dp"), None),
        P(),
        P(),
        P(),
        P(),
        P(),
        P(),
        P(),
        P(),
        P(),
        P(),
        P(),
        P(),
        P(("half", "dp"), None),
    )
    out_specs = (
        P(("half", "dp"), None),
        P(("half", "dp"), None),
        P(("half", "dp"), None),
        P(("half", "dp"), None),
        P(("half", "dp")),
        P(("half", "dp")),
        P(("half", "dp")),
        P(("half", "dp"), None),
        P(("half", "dp"), None),
        P(("half", "dp")),
        P(("half", "dp")),
        P(("half", "dp"), None),
        P(("half", "dp")),
        P(("half", "dp"), None),
        P(("half", "dp")),
    )
    return jax.shard_map(
        on_device, mesh=mesh, in_specs=in_specs, out_specs=out_specs, check_vma=False
    )
```

```python
import functools

import jax
import jax.numpy as jnp
from jax import lax
from jax.experimental import pallas as pl
from jax.experimental.pallas import tpu as pltpu
from jax.sharding import PartitionSpec as P

D = 1024
H = 16
HD = 64
ROW_LEN = 1024
BLOCK = 128
BLOCKS = ROW_LEN // BLOCK
TILE = 256
HEADS = 8
GROUPS = H // HEADS
FAR = 1e30
epsilon = 1e-05
f32 = jnp.float32
bf16 = jnp.bfloat16
MIB = 1024 * 1024


def nn(left, right):
    return jnp.dot(left, right, preferred_element_type=f32)


def nt(left, right):
    return lax.dot_general(left, right, (((1,), (1,)), ((), ())), preferred_element_type=f32)


def tn(left, right):
    return lax.dot_general(left, right, (((0,), (0,)), ((), ())), preferred_element_type=f32)


def settings(megabytes):
    return pltpu.CompilerParams(vmem_limit_bytes=megabytes * MIB)


def cost(flops, moved):
    return pl.CostEstimate(flops=int(flops), bytes_accessed=int(moved), transcendentals=0)


def held(shape):
    zeros = (0,) * len(shape)
    return pl.BlockSpec(shape, lambda *_: zeros, pipeline_mode=pl.Buffered(1))


def tiled(columns):
    return pl.BlockSpec((TILE, columns), lambda i: (i, 0))


def summed_over(columns):
    return pl.BlockSpec((1, columns), lambda i: (0, 0))


def swapped(value, axis, apart):
    mask = 2**apart
    pairs = [(source, source ^ mask) for source in range(lax.axis_size(axis))]
    return lax.ppermute(value, axis, pairs)


def mesh_bits():
    dp_bits = lax.axis_size("dp").bit_length() - 1
    half_bits = lax.axis_size("half").bit_length() - 1
    return [("half", bit) for bit in reversed(range(half_bits))] + [
        ("dp", bit) for bit in reversed(range(dp_bits))
    ]


def halve(block, left, order, kept_type):
    bits = mesh_bits()
    left = list(left)
    for step, digit in enumerate(order):
        axis, apart = bits[digit]
        mine = (lax.axis_index(axis) >> apart) & 1
        at = left.index(digit)
        left.pop(at)
        sent = lax.dynamic_index_in_dim(block, 1 - mine, at, keepdims=False)
        kept = lax.dynamic_index_in_dim(block, mine, at, keepdims=False)
        got = swapped(sent, axis, apart)
        block = kept.astype(f32) + got.astype(f32)
        if step < len(order) - 1:
            block = block.astype(kept_type)
    return block


def digits():
    count = len(mesh_bits())
    core, second = count - 1, count - 2
    return core, 0, second, list(range(second - 1, 0, -1))


def reduced(pair, first):
    count = len(mesh_bits())
    sent, kept = pair
    core, x, y, rest = digits()
    got = swapped(sent, "dp", 0)
    block = (kept.astype(f32) + got.astype(f32)).astype(bf16)
    rows, columns = block.shape
    block = block.reshape((2,) * (count - 1) + (rows >> (count - 1), columns))
    orders = {"x": [x, y] + rest, "y": [y, x] + rest, "z": rest + [y, x]}
    if len(first) == 1:
        return halve(block, range(count - 1), orders[first], bf16)
    cut = columns // 2
    return jnp.concatenate(
        [
            halve(block[..., :cut], range(count - 1), orders[first[0]], bf16),
            halve(block[..., cut:], range(count - 1), orders[first[1]], bf16),
        ],
        axis=1,
    )


def reduced_vectors(vectors):
    count = len(mesh_bits())
    core, x, y, rest = digits()
    parts = [vector.reshape(1 << count, -1) for vector in vectors]
    joined = jnp.concatenate(parts, axis=1)
    total = halve(
        joined.reshape((2,) * count + (joined.shape[1],)), range(count), [core, x, y] + rest, f32
    )
    cuts = []
    start = 0
    for part in parts:
        cuts.append(total[start : start + part.shape[1]])
        start += part.shape[1]
    return cuts


def split_rows(total, core, rows_each):
    rows, columns = total.shape
    cut = total.reshape(rows // (2 * rows_each), 2, rows_each, columns)
    first, second = cut[:, 0], cut[:, 1]
    even = core == 0
    sent = jnp.where(even, second, first).reshape(rows // 2, columns)
    kept = jnp.where(even, first, second).reshape(rows // 2, columns)
    return sent.astype(bf16), kept.astype(bf16)


def row_stats(values):
    mean = jnp.mean(values, axis=-1, keepdims=True)
    centred = values - mean
    scale = lax.rsqrt(jnp.mean(centred * centred, axis=-1, keepdims=True) + epsilon)
    return centred * scale, scale


def norm_back(values, gain, grad):
    normal, scale = row_stats(values)
    inner = grad * gain
    along = jnp.mean(inner * normal, axis=-1, keepdims=True)
    return scale * (inner - jnp.mean(inner, axis=-1, keepdims=True) - normal * along), grad * normal


def add_rows(out_ref, values):
    @pl.when(pl.program_id(0) == 0)
    def _():
        out_ref[...] = jnp.zeros_like(out_ref)

    out_ref[...] += jnp.sum(values, axis=0, keepdims=True)


def enter_kernel(part, mirror, merge, gain, shift, qkv, hidden, normed, projected):
    value = part[...] + nn(mirror[...], merge[...])
    hidden[...] = value
    low = (row_stats(value)[0] * gain[...] + shift[...]).astype(bf16)
    normed[...] = low
    projected[...] = nn(low, qkv[...]).astype(bf16)


def enter(part, mirror, merge_low, gain, shift, qkv):
    tokens = part.shape[0]
    return pl.pallas_call(
        enter_kernel,
        grid=(tokens // TILE,),
        in_specs=[tiled(D), tiled(D), held((D, D)), held((1, D)), held((1, D)), held((D, 3 * D))],
        out_specs=[tiled(D), tiled(D), tiled(3 * D)],
        out_shape=[
            jax.ShapeDtypeStruct((tokens, D), f32),
            jax.ShapeDtypeStruct((tokens, D), bf16),
            jax.ShapeDtypeStruct((tokens, 3 * D), bf16),
        ],
        compiler_params=settings(40),
        cost_estimate=cost(8 * tokens * D * D, 26 * MIB),
        name="enter",
    )(part, mirror, merge_low, gain, shift, qkv)


def leave_kernel(hidden, mixed, out_weight, gain, shift, residual, normed):
    value = hidden[...] + nn(mixed[...], out_weight[...])
    residual[...] = value
    normed[...] = (row_stats(value)[0] * gain[...] + shift[...]).astype(bf16)


def leave(hidden, mixed, out_weight, gain, shift):
    tokens = hidden.shape[0]
    return pl.pallas_call(
        leave_kernel,
        grid=(tokens // TILE,),
        in_specs=[tiled(D), tiled(D), held((D, D)), held((1, D)), held((1, D))],
        out_specs=[tiled(D), tiled(D)],
        out_shape=[jax.ShapeDtypeStruct((tokens, D), f32), jax.ShapeDtypeStruct((tokens, D), bf16)],
        compiler_params=settings(32),
        cost_estimate=cost(2 * tokens * D * D, 14 * MIB),
        name="leave",
    )(hidden, mixed, out_weight, gain, shift)


def windows(lengths):
    ends = jnp.cumsum(lengths, axis=1)
    starts = ends - lengths
    low = (jnp.arange(BLOCKS, dtype=jnp.int32) * BLOCK)[None, :, None]
    holds_low = (low >= starts[:, None, :]) & (low < ends[:, None, :])
    high = low + (BLOCK - 1)
    holds_high = (high >= starts[:, None, :]) & (high < ends[:, None, :])
    window_low = jnp.sum(jnp.where(holds_low, starts[:, None, :], 0), axis=2) // BLOCK
    window_high = (jnp.sum(jnp.where(holds_high, ends[:, None, :], 0), axis=2) + BLOCK - 1) // BLOCK
    return window_low.reshape(-1), (window_high - window_low).reshape(-1)


def row_segments(lengths):
    ends = jnp.cumsum(lengths, axis=1)
    position = jnp.arange(ROW_LEN, dtype=jnp.int32)
    return jnp.sum((position[None, :, None] >= ends[:, None, :]).astype(jnp.int32), axis=2)


def head_slopes():
    return jnp.array([2.0 ** (-8.0 * (head + 1.0) / H) for head in range(H)], f32)


def fill_distance(far_ref, column, line):
    for b in range(BLOCKS):
        rows = slice(b * BLOCK, (b + 1) * BLOCK)
        i = lax.broadcasted_iota(jnp.int32, (BLOCK, ROW_LEN), 0) + b * BLOCK
        j = lax.broadcasted_iota(jnp.int32, (BLOCK, ROW_LEN), 1)
        distance = jnp.abs(i - j).astype(f32)
        far_ref[rows, :] = jnp.where(column[rows, :] == line[...], distance, FAR)


def masked_pair(value, lows):
    zero = jnp.zeros_like(value)
    return jnp.concatenate([jnp.where(lows, value, zero), jnp.where(lows, zero, value)], axis=0)


def over_blocks(low_ref, count_ref, row, variant):
    def block(b, carry):
        rows = pl.ds(pl.multiple_of(b * BLOCK, BLOCK), BLOCK)
        start = pl.multiple_of(low_ref[row * BLOCKS + b] * BLOCK, BLOCK)
        count = count_ref[row * BLOCKS + b]
        for n in range(1, BLOCKS + 1):
            pl.when(count == n)(functools.partial(variant, rows, pl.ds(start, n * BLOCK)))
        return carry

    lax.fori_loop(0, BLOCKS, block, 0)


def attend_kernel(
    low_ref, count_ref, slope_ref, column, line, q_ref, k_ref, v_ref, o_ref, lse_ref, far_ref, value_ref
):
    row = pl.program_id(0)
    group = pl.program_id(1)

    @pl.when(group == 0)
    def _():
        fill_distance(far_ref, column, line)
        lse_ref[...] = jnp.zeros_like(lse_ref)

    lane = lax.broadcasted_iota(jnp.int32, (1, 128), 1)
    lows = lane < HD
    for pair in range(HEADS // 2):
        value_ref[pair, :, :128] = v_ref[:, pair * 128 : pair * 128 + 128]
        value_ref[pair, :, 128:] = jnp.ones((ROW_LEN, 128), bf16)

    def variant(rows, cols):
        far = far_ref[rows, cols]
        logs = lse_ref[rows, :]
        for pair in range(HEADS // 2):
            at = slice(pair * 128, pair * 128 + 128)
            head = group * HEADS + pair * 2
            query = masked_pair(q_ref[rows, at] * bf16(HD**-0.5), lows)
            score = nt(query, k_ref[cols, at])
            score = score - jnp.concatenate([slope_ref[head] * far, slope_ref[head + 1] * far], axis=0)
            top = jnp.max(score, axis=1, keepdims=True)
            soft = jnp.exp(score - top).astype(bf16)
            both = nn(soft, value_ref[pair, cols, :])
            total = both[:, 128:]
            log_total = top + jnp.log(total)
            logs = jnp.where(lane == head, log_total[:BLOCK], logs)
            logs = jnp.where(lane == head + 1, log_total[BLOCK:], logs)
            mixed = jnp.where(lows, both[:BLOCK, :128], both[BLOCK:, :128])
            o_ref[rows, at] = (mixed / jnp.where(lows, total[:BLOCK], total[BLOCK:])).astype(bf16)
        lse_ref[rows, :] = logs

    over_blocks(low_ref, count_ref, row, variant)


def head_group(part):
    return pl.BlockSpec((ROW_LEN, HEADS * HD), lambda r, g, *_: (r, part * GROUPS + g))


def attention_operands(lengths):
    rows = lengths.shape[0]
    segments = row_segments(lengths)
    return windows(lengths) + (
        head_slopes(),
        segments.reshape(rows * ROW_LEN, 1),
        segments.reshape(rows, 1, ROW_LEN),
    )


def segment_specs():
    return [
        pl.BlockSpec((ROW_LEN, 1), lambda r, g, *_: (r, 0)),
        pl.BlockSpec((None, 1, ROW_LEN), lambda r, g, *_: (r, 0, 0)),
    ]


def attend(projected, operands):
    tokens = projected.shape[0]
    rows = tokens // ROW_LEN
    return pl.pallas_call(
        attend_kernel,
        out_shape=[jax.ShapeDtypeStruct((tokens, D), bf16), jax.ShapeDtypeStruct((tokens, 128), f32)],
        grid_spec=pltpu.PrefetchScalarGridSpec(
            num_scalar_prefetch=3,
            grid=(rows, GROUPS),
            in_specs=segment_specs() + [head_group(0), head_group(1), head_group(2)],
            out_specs=[head_group(0), pl.BlockSpec((ROW_LEN, 128), lambda r, g, *_: (r, 0))],
            scratch_shapes=[
                pltpu.VMEM((ROW_LEN, ROW_LEN), f32),
                pltpu.VMEM((HEADS // 2, ROW_LEN, 256), bf16),
            ],
        ),
        compiler_params=settings(48),
        cost_estimate=cost(rows * 20e9, 30 * MIB),
        name="attend",
    )(*operands, projected, projected, projected)


def attend_back_kernel(
    low_ref,
    count_ref,
    slope_ref,
    column,
    line,
    q_ref,
    k_ref,
    v_ref,
    grad_ref,
    lse_ref,
    delta_ref,
    out_ref,
    far_ref,
    turned_ref,
    key_ref,
):
    row = pl.program_id(0)
    group = pl.program_id(1)

    @pl.when(group == 0)
    def _():
        fill_distance(far_ref, column, line)

    lows = lax.broadcasted_iota(jnp.int32, (1, 128), 1) < HD
    tops = lax.broadcasted_iota(jnp.int32, (128, 1), 0) < HD
    turned_ref[...] = jnp.zeros_like(turned_ref)
    for pair in range(HEADS // 2):
        key_ref[pair] = k_ref[:, pair * 128 : pair * 128 + 128].T

    def variant(rows, cols):
        far = far_ref[rows, cols]
        for pair in range(HEADS // 2):
            at = slice(pair * 128, pair * 128 + 128)
            head = group * HEADS + pair * 2
            query = q_ref[cols, at] * bf16(HD**-0.5)
            grad = grad_ref[cols, at]
            score = nt(masked_pair(k_ref[rows, at], lows), query)
            soft_grad = nt(masked_pair(v_ref[rows, at], lows), grad)
            softs, score_grads = [], []
            for side in range(2):
                part = slice(side * BLOCK, side * BLOCK + BLOCK)
                own = pl.ds(pair * 2 + side, 1)
                soft = jnp.exp(score[part] - slope_ref[head + side] * far - lse_ref[own, cols])
                score_grads.append((soft * (soft_grad[part] - delta_ref[own, cols])).astype(bf16))
                softs.append(soft.astype(bf16))
            score_grad = jnp.concatenate(score_grads, axis=0)
            value_grad = nn(jnp.concatenate(softs, axis=0), grad)
            key_grad = nn(score_grad, query)
            out_ref[2, rows, at] = jnp.where(lows, value_grad[:BLOCK], value_grad[BLOCK:]).astype(bf16)
            out_ref[1, rows, at] = jnp.where(lows, key_grad[:BLOCK], key_grad[BLOCK:]).astype(bf16)
            key = key_ref[pair, :, rows]
            zero = jnp.zeros_like(key)
            keys = jnp.concatenate([jnp.where(tops, key, zero), jnp.where(tops, zero, key)], axis=1)
            turned_ref[at, cols] += nn(keys, score_grad)

    over_blocks(low_ref, count_ref, row, variant)
    out_ref[0] = (turned_ref[...].T * HD**-0.5).astype(bf16)


def attend_back(projected, grad, lse_rows, delta_rows, operands):
    tokens = projected.shape[0]
    rows = tokens // ROW_LEN
    thin = pl.BlockSpec((None, HEADS, ROW_LEN), lambda r, g, *_: (r, g, 0))
    return pl.pallas_call(
        attend_back_kernel,
        out_shape=jax.ShapeDtypeStruct((3, tokens, D), bf16),
        grid_spec=pltpu.PrefetchScalarGridSpec(
            num_scalar_prefetch=3,
            grid=(rows, GROUPS),
            in_specs=segment_specs()
            + [head_group(0), head_group(1), head_group(2), head_group(0), thin, thin],
            out_specs=pl.BlockSpec((3, ROW_LEN, HEADS * HD), lambda r, g, *_: (0, r, g)),
            scratch_shapes=[
                pltpu.VMEM((ROW_LEN, ROW_LEN), f32),
                pltpu.VMEM((HEADS * HD, ROW_LEN), f32),
                pltpu.VMEM((HEADS // 2, 128, ROW_LEN), bf16),
            ],
        ),
        compiler_params=settings(48),
        cost_estimate=cost(rows * 30e9, 30 * MIB),
        name="attend_back",
    )(*operands, projected, projected, projected, grad, lse_rows, delta_rows)


PULL = 0.44
ERFC = (
    0.1241083994,
    0.1244657618,
    0.1084788423,
    0.1084610390,
    -0.0110834557,
    0.1493682951,
    -0.1395405297,
    0.0357417408,
)


def gelu_pair(value):
    size = jnp.abs(value)
    t = 1.0 / (1.0 + (PULL * 0.5**0.5) * size)
    poly = jnp.full_like(t, ERFC[-1])
    for term in reversed(ERFC[:-1]):
        poly = poly * t + term
    bell = jnp.exp(value * value * -0.5)
    tail = bell * t * poly
    whole = jnp.where(value < 0, tail, 1.0 - tail)
    return value * whole, whole + value * (bell * (0.5 / jnp.pi) ** 0.5)


def feed_kernel(
    rows_up,
    rows_down,
    core_ref,
    normed,
    cotangent,
    residual,
    down_bias,
    up_weight,
    up_bias,
    down_weight,
    back,
    output,
    normed_grad,
    bias_grad,
    up_sent,
    up_kept,
    down_sent,
    down_kept,
    total,
):
    step = pl.program_id(0)
    core = core_ref[0]

    @pl.when(step == 0)
    def _():
        total[...] = residual[...] + down_bias[...]
        normed_grad[...] = jnp.zeros_like(normed_grad)

    value = nn(normed[...], up_weight[...]) + up_bias[...]
    active, slope = gelu_pair(value)
    active = active.astype(bf16)
    grad = (back[...].astype(f32) * slope).astype(bf16)
    bias_grad[...] = jnp.sum(grad.astype(f32), axis=0, keepdims=True)
    total[...] += nn(active, down_weight[...])
    normed_grad[...] += nt(grad, up_weight[...])
    down_sent[...], down_kept[...] = split_rows(tn(active, cotangent[...]), core, rows_down)
    up_sent[...], up_kept[...] = split_rows(tn(normed[...], grad), core, rows_up)

    @pl.when(step == pl.num_programs(0) - 1)
    def _():
        output[...] = total[...].astype(bf16)


def feed(core, normed, cotangent, residual, down_bias, up_weight, up_bias, down_weight, back, width=512):
    tokens = normed.shape[0]
    hidden_units = up_weight.shape[1]
    devices = lax.axis_size("half") * lax.axis_size("dp")
    across = lambda rows: pl.BlockSpec((rows, width), lambda i: (0, i))
    down = lambda rows: pl.BlockSpec((rows, D), lambda i: (i, 0))
    shape = jax.ShapeDtypeStruct
    return pl.pallas_call(
        functools.partial(feed_kernel, D // devices, hidden_units // devices),
        grid=(hidden_units // width,),
        in_specs=[
            pl.BlockSpec(memory_space=pltpu.SMEM),
            held((tokens, D)),
            held((tokens, D)),
            held((tokens, D)),
            held((1, D)),
            across(D),
            across(1),
            down(width),
            across(tokens),
        ],
        out_specs=[
            pl.BlockSpec((tokens, D), lambda i: (0, 0)),
            pl.BlockSpec((tokens, D), lambda i: (0, 0)),
            across(1),
            across(D // 2),
            across(D // 2),
            down(width // 2),
            down(width // 2),
        ],
        out_shape=[
            shape((tokens, D), bf16),
            shape((tokens, D), f32),
            shape((1, hidden_units), f32),
            shape((D // 2, hidden_units), bf16),
            shape((D // 2, hidden_units), bf16),
            shape((hidden_units // 2, D), bf16),
            shape((hidden_units // 2, D), bf16),
        ],
        scratch_shapes=[pltpu.VMEM((tokens, D), f32)],
        compiler_params=settings(60),
        cost_estimate=cost(10 * tokens * D * hidden_units, 60 * MIB),
        name="feed",
    )(core, normed, cotangent, residual, down_bias, up_weight, up_bias, down_weight, back)


def second_back_kernel(
    normed_grad,
    residual,
    cotangent,
    gain,
    out_weight,
    mixed,
    lse,
    residual_grad,
    attention_grad,
    mixed_grad,
    delta_rows,
    lse_rows,
    gain_grad,
    shift_grad,
    bias_grad,
):
    incoming = normed_grad[...]
    outer = cotangent[...].astype(f32)
    through, gain_terms = norm_back(residual[...], gain[...], incoming)
    value = outer + through
    residual_grad[...] = value
    low = value.astype(bf16)
    attention_grad[...] = low
    mixed_low = nt(low, out_weight[...]).astype(bf16)
    mixed_grad[...] = mixed_low
    product = mixed_low.astype(f32) * mixed[...].astype(f32)
    high = product.astype(bf16)
    rest = (product - high.astype(f32)).astype(bf16)
    of_head = lax.broadcasted_iota(jnp.int32, (H, D), 1) // HD
    member = (of_head == lax.broadcasted_iota(jnp.int32, (H, D), 0)).astype(bf16)
    delta_rows[...] = nt(member, high) + nt(member, rest)
    lse_rows[...] = lse[...].T[:H]
    add_rows(gain_grad, gain_terms)
    add_rows(shift_grad, incoming)
    add_rows(bias_grad, outer)


def second_back(normed_grad, residual, cotangent, gain, out_weight, mixed, lse):
    tokens = residual.shape[0]
    per_row = ROW_LEN // TILE
    shape = jax.ShapeDtypeStruct
    thin = pl.BlockSpec((None, H, TILE), lambda i: (i // per_row, 0, i % per_row))
    return pl.pallas_call(
        second_back_kernel,
        grid=(tokens // TILE,),
        in_specs=[tiled(D), tiled(D), tiled(D), held((1, D)), held((D, D)), tiled(D), tiled(128)],
        out_specs=[tiled(D), tiled(D), tiled(D), thin, thin, summed_over(D), summed_over(D), summed_over(D)],
        out_shape=[
            shape((tokens, D), f32),
            shape((tokens, D), bf16),
            shape((tokens, D), bf16),
            shape((tokens // ROW_LEN, H, ROW_LEN), f32),
            shape((tokens // ROW_LEN, H, ROW_LEN), f32),
            shape((1, D), f32),
            shape((1, D), f32),
            shape((1, D), f32),
        ],
        compiler_params=settings(40),
        cost_estimate=cost(3 * tokens * D * D, 22 * MIB),
        name="second_back",
    )(normed_grad, residual, cotangent, gain, out_weight, mixed, lse)


def first_back_kernel(
    projected_grad, hidden, residual_grad, gain, qkv, merge, hidden_grad, frames_grad, skip_grad, gain_grad, shift_grad, bias_grad
):
    incoming = nt(projected_grad[0], qkv[:, :D])
    incoming += nt(projected_grad[1], qkv[:, D : 2 * D])
    incoming += nt(projected_grad[2], qkv[:, 2 * D :])
    through, gain_terms = norm_back(hidden[...], gain[...], incoming)
    low = (residual_grad[...] + through).astype(bf16)
    hidden_grad[...] = low
    skip_grad[...] = nt(low, merge[D:, :]).astype(bf16)
    frames_grad[...] = nt(low, merge[:D, :]).astype(bf16)
    add_rows(gain_grad, gain_terms)
    add_rows(shift_grad, incoming)
    add_rows(bias_grad, low.astype(f32))


def first_back(projected_grad, hidden, residual_grad, gain, qkv, merge):
    tokens = hidden.shape[0]
    shape = jax.ShapeDtypeStruct
    return pl.pallas_call(
        first_back_kernel,
        grid=(tokens // TILE,),
        in_specs=[
            pl.BlockSpec((3, TILE, D), lambda i: (0, i, 0)),
            tiled(D),
            tiled(D),
            held((1, D)),
            held((D, 3 * D)),
            held((2 * D, D)),
        ],
        out_specs=[tiled(D), tiled(D), tiled(D), summed_over(D), summed_over(D), summed_over(D)],
        out_shape=[shape((tokens, D), bf16)] * 3 + [shape((1, D), f32)] * 3,
        compiler_params=settings(48),
        cost_estimate=cost(10 * tokens * D * D, 32 * MIB),
        name="first_back",
    )(projected_grad, hidden, residual_grad, gain, qkv, merge)


def weight_kernel(rows_each, core_ref, left, right, sent, kept):
    sent[...], kept[...] = split_rows(tn(left[...], right[...]), core_ref[0], rows_each)


def weight_pair_kernel(rows_each, core_ref, first, second, right, sent, kept):
    half = sent.shape[0] // 2
    for at, left in enumerate((first, second)):
        rows = slice(at * half, at * half + half)
        sent[rows, :], kept[rows, :] = split_rows(tn(left[...], right[...]), core_ref[0], rows_each)


def weight_grad(core, lefts, right, right_spec, steps, width, name):
    tokens = lefts[0].shape[0]
    devices = lax.axis_size("half") * lax.axis_size("dp")
    rows = len(lefts) * D
    kernel = weight_kernel if len(lefts) == 1 else weight_pair_kernel
    out = pl.BlockSpec((rows // 2, width), lambda i: (0, i))
    return pl.pallas_call(
        functools.partial(kernel, rows // devices),
        grid=(steps,),
        in_specs=[pl.BlockSpec(memory_space=pltpu.SMEM)] + [held((tokens, D))] * len(lefts) + [right_spec],
        out_specs=[out, out],
        out_shape=[jax.ShapeDtypeStruct((rows // 2, steps * width), bf16)] * 2,
        compiler_params=settings(48),
        cost_estimate=cost(2 * tokens * rows * steps * width, 16 * MIB),
        name=name,
    )(core, *lefts, right)


def columns_of(tokens, width):
    return pl.BlockSpec((tokens, width), lambda i: (0, i))


def on_device(
    frames,
    skip_rows,
    lengths,
    merge_weight,
    merge_bias,
    norm1_gain,
    norm1_bias,
    qkv_weight,
    out_weight,
    norm2_gain,
    norm2_bias,
    up_weight,
    up_bias,
    down_weight,
    down_bias,
    cotangent,
):
    tokens = frames.shape[0]
    line = lambda vector: vector.reshape(1, -1)
    core = (lax.axis_index("dp") & 1).astype(jnp.int32).reshape(1)
    mirror = swapped(skip_rows, "half", 0)
    operands = attention_operands(lengths)
    back = nt(cotangent, down_weight).astype(bf16)
    part = nn(frames, merge_weight[:D]) + merge_bias
    hidden, normed, projected = enter(
        part, mirror, merge_weight[D:], line(norm1_gain), line(norm1_bias), qkv_weight
    )
    mixed, lse = attend(projected, operands)
    residual, normed_two = leave(hidden, mixed, out_weight, line(norm2_gain), line(norm2_bias))
    output, normed_two_grad, up_bias_grad, up_sent, up_kept, down_sent, down_kept = feed(
        core, normed_two, cotangent, residual, line(down_bias), up_weight, line(up_bias), down_weight, back
    )
    down_weight_grad = reduced((down_sent, down_kept), "x")
    up_weight_grad = reduced((up_sent, up_kept), "y")
    residual_grad, attention_grad, mixed_grad, delta_rows, lse_rows, gain_two, shift_two, down_bias_grad = (
        second_back(normed_two_grad, residual, cotangent, line(norm2_gain), out_weight, mixed, lse)
    )
    out_weight_grad = reduced(
        weight_grad(core, (mixed,), attention_grad, columns_of(tokens, 512), 2, 512, "out_grad"), "x"
    )
    projected_grad = attend_back(projected, mixed_grad, lse_rows, delta_rows, operands)
    hidden_grad, frames_grad, skip_part, gain_one, shift_one, merge_bias_grad = first_back(
        projected_grad, hidden, residual_grad, line(norm1_gain), qkv_weight, merge_weight
    )
    skip_grad = swapped(skip_part, "half", 0)
    third = pl.BlockSpec((None, tokens, D), lambda i: (i, 0, 0))
    qkv_weight_grad = reduced(weight_grad(core, (normed,), projected_grad, third, 3, D, "qkv_grad"), "yz")
    merge_weight_grad = reduced(
        weight_grad(core, (frames, mirror), hidden_grad, columns_of(tokens, 512), 2, 512, "merge_grad"), "yz"
    )
    vectors = reduced_vectors(
        (merge_bias_grad, gain_one, shift_one, gain_two, shift_two, up_bias_grad, down_bias_grad)
    )
    return (
        output,
        frames_grad,
        skip_grad,
        merge_weight_grad,
        vectors[0],
        vectors[1],
        vectors[2],
        qkv_weight_grad,
        out_weight_grad,
        vectors[3],
        vectors[4],
        up_weight_grad,
        vectors[5],
        down_weight_grad,
        vectors[6],
    )


def solution(mesh):
    rows = P(("half", "dp"), None)
    parts = P(("half", "dp"))
    in_specs = (rows, rows, rows) + (P(),) * 12 + (rows,)
    out_specs = (rows, rows, rows, rows, parts, parts, parts, rows, rows, parts, parts, rows, parts, rows, parts)
    return jax.shard_map(
        on_device, mesh=mesh, in_specs=in_specs, out_specs=out_specs, check_vma=False
    )
```

```python
import functools

import jax
import jax.numpy as jnp
from jax import lax
from jax.experimental import pallas as pl
from jax.experimental.pallas import tpu as pltpu
from jax.sharding import PartitionSpec as P

D = 1024
H = 16
HD = 64
ROW_LEN = 1024
BLOCK = 128
BLOCKS = ROW_LEN // BLOCK
TILE = 256
CUTS = (0, 768, 1024)
VMEM_MIB = 48
LANES = 512
VECTOR_ROWS = 16
SKIP_CUTS = (0, 512, 1024)
HEADS = 8
GROUPS = H // HEADS
FAR = 1e30
epsilon = 1e-05
f32 = jnp.float32
bf16 = jnp.bfloat16
MIB = 1024 * 1024


def nn(left, right):
    return jnp.dot(left, right, preferred_element_type=f32)


def nt(left, right):
    return lax.dot_general(left, right, (((1,), (1,)), ((), ())), preferred_element_type=f32)


def tn(left, right):
    return lax.dot_general(left, right, (((0,), (0,)), ((), ())), preferred_element_type=f32)


def settings(**more):
    return pltpu.CompilerParams(vmem_limit_bytes=VMEM_MIB * MIB, **more)


def cost(flops, moved):
    return pl.CostEstimate(flops=int(flops), bytes_accessed=int(moved), transcendentals=0)


def held(shape):
    zeros = (0,) * len(shape)
    return pl.BlockSpec(shape, lambda *_: zeros, pipeline_mode=pl.Buffered(1))


def tiled(columns):
    return pl.BlockSpec((TILE, columns), lambda i: (i, 0))


def summed_over(columns):
    return pl.BlockSpec((8, columns), lambda i: (0, 0))


def launch(kernel, operands, pins=(), in_specs=(), scalars=0, **rest):
    count, extra = len(operands), len(pins)

    def body(*refs):
        kernel(*refs[:count], *refs[count + extra :])

    in_specs = list(in_specs) + [pl.BlockSpec(memory_space=pl.ANY)] * extra
    if scalars:
        rest["grid_spec"] = pltpu.PrefetchScalarGridSpec(
            num_scalar_prefetch=scalars,
            grid=rest.pop("grid"),
            in_specs=in_specs,
            out_specs=rest.pop("out_specs"),
            scratch_shapes=rest.pop("scratch_shapes"),
        )
    else:
        rest["in_specs"] = in_specs
    return pl.pallas_call(body, **rest)(*operands, *pins)


def swapped(value, axis, apart):
    mask = 2**apart
    pairs = [(source, source ^ mask) for source in range(lax.axis_size(axis))]
    return lax.ppermute(value, axis, pairs)


def mesh_bits():
    dp_bits = lax.axis_size("dp").bit_length() - 1
    half_bits = lax.axis_size("half").bit_length() - 1
    return [("half", bit) for bit in reversed(range(half_bits))] + [
        ("dp", bit) for bit in reversed(range(dp_bits))
    ]


def digits():
    count = len(mesh_bits())
    return count - 1, 0, count - 2, list(range(count - 3, 0, -1))


def my_sides():
    return jnp.stack([(lax.axis_index(axis) >> apart) & 1 for axis, apart in mesh_bits()]).astype(jnp.int32)


class Piece:
    def __init__(self, left, rows, kept, got=None, offset=0):
        self.left, self.rows, self.kept, self.got, self.offset = tuple(left), rows, kept, got, offset


def started(sent, kept):
    count = len(mesh_bits()) - 1
    flat = lambda value: value.reshape(-1, LANES)
    kept = flat(kept)
    return Piece(range(count), kept.shape[0] >> count, kept, swapped(flat(sent), "dp", 0))


def mix_kernel(plan, loaded, sides_ref, *refs):
    for take in plan:
        low = take["bits"]
        rows, whole = take["rows"], take["whole"]
        kept_in, got_in = refs[take["kept"]], refs[take["got"]]
        for to, offset, other in ((take["to_sent"], take["sent_at"], True), (take["to_kept"], 0, False)):
            side = sides_ref[take["digit"]]
            side = 1 - side if other else side
            out = refs[loaded + to]

            def one(at, carry, side=side, out=out, offset=offset, take=take, low=low, rows=rows, whole=whole):
                block = ((((at >> low) * 2) + side) << low) + (at & ((1 << low) - 1))
                start = block * whole + take["first"]
                mine = refs[take["kept"]][pl.ds(pl.multiple_of(start, 8), rows), :]
                theirs = refs[take["got"]][pl.ds(pl.multiple_of(take["got_at"] + start, 8), rows), :]
                total = mine.astype(f32) + theirs.astype(f32)
                out[pl.ds(pl.multiple_of(offset + at * rows, 8), rows), :] = total.astype(bf16)
                return carry

            lax.fori_loop(0, take["blocks"], one, 0)


def whole_of(array):
    zeros = (0,) * array.ndim
    return pl.BlockSpec(array.shape, lambda *_: zeros)


def place_in(arrays, array):
    for at, known in enumerate(arrays):
        if known is array:
            return at
    arrays.append(array)
    return len(arrays) - 1


def mix(parts):
    arrays, plan, shapes, pieces = [], [], [], []
    bundles = {}
    for piece, cuts in parts:
        for first, last, digit in cuts:
            rows = last - first
            at = piece.left.index(digit)
            left = piece.left[:at] + piece.left[at + 1 :]
            blocks = 1 << len(left)
            plan.append(
                dict(
                    kept=place_in(arrays, piece.kept),
                    got=place_in(arrays, piece.got),
                    got_at=piece.offset,
                    whole=piece.rows,
                    first=first,
                    rows=rows,
                    blocks=blocks,
                    bits=len(left) - at,
                    digit=digit,
                    to_kept=len(pieces),
                    sent_at=bundles.get(digit, 0),
                )
            )
            pieces.append(Piece(left, rows, None, None, bundles.get(digit, 0)))
            shapes.append((blocks * rows, LANES))
            bundles[digit] = bundles.get(digit, 0) + blocks * rows
    links = list(bundles)
    for take in plan:
        take["to_sent"] = len(pieces) + links.index(take["digit"])
    shapes = shapes + [(bundles[digit], LANES) for digit in links]
    outs = [jax.ShapeDtypeStruct(shape, bf16) for shape in shapes]
    results = pl.pallas_call(
        functools.partial(mix_kernel, plan, len(arrays)),
        in_specs=[pl.BlockSpec(memory_space=pltpu.SMEM)] + [whole_of(array) for array in arrays],
        out_specs=[whole_of(out) for out in outs],
        out_shape=outs,
        compiler_params=settings(),
        cost_estimate=cost(1e6, 4 * sum(shape[0] for shape in shapes) * LANES),
        name="mix",
    )(my_sides(), *arrays)
    arrived = {}
    for digit, sent in zip(links, results[len(pieces) :]):
        axis, apart = mesh_bits()[digit]
        arrived[digit] = swapped(sent, axis, apart)
    for take, piece, kept in zip(plan, pieces, results):
        piece.kept, piece.got = kept, arrived[take["digit"]]
    return pieces


def finish_kernel(plan, loaded, *refs):
    for take in plan:
        first, rows = take["first"], take["rows"]
        start = take["got_at"] + first
        total = refs[take["kept"]][first : first + rows, :].astype(f32) + refs[take["got"]][
            start : start + rows, :
        ].astype(f32)
        column = take["column"]
        refs[loaded + take["out"]][:, column : column + LANES] = total


def finish(shapes, panels):
    arrays, plan = [], []
    for piece, first, out, column in panels:
        plan.append(
            dict(
                kept=place_in(arrays, piece.kept),
                got=place_in(arrays, piece.got),
                got_at=piece.offset,
                first=first,
                rows=shapes[out][0],
                out=out,
                column=column,
            )
        )
    outs = [jax.ShapeDtypeStruct(shape, f32) for shape in shapes]
    return pl.pallas_call(
        functools.partial(finish_kernel, plan, len(arrays)),
        in_specs=[whole_of(array) for array in arrays],
        out_specs=[whole_of(out) for out in outs],
        out_shape=outs,
        compiler_params=settings(),
        cost_estimate=cost(1e6, 8e6),
        name="finish",
    )(*arrays)


def vector_piece(vectors):
    count = len(mesh_bits())
    devices = 1 << count
    values = jnp.concatenate([vector.reshape(devices, -1) for vector in vectors], axis=1).astype(bf16)
    values = jnp.pad(values[:, None, :], ((0, 0), (0, VECTOR_ROWS - 1), (0, LANES - values.shape[1])))
    values = values.reshape(devices // 2, 2, VECTOR_ROWS, LANES)
    mine = lax.axis_index("dp") & 1
    return started(
        lax.dynamic_index_in_dim(values, 1 - mine, 1, keepdims=False),
        lax.dynamic_index_in_dim(values, mine, 1, keepdims=False),
    )


class Sent:
    def __init__(self, value, axis, apart):
        self.got = swapped(value, axis, apart)


def in_order(values, arrived=(), ready=()):
    gots = []
    for piece in arrived:
        place_in(gots, piece.got)
    kepts = tuple(piece.kept for piece in ready)
    tied = lax.optimization_barrier((tuple(values), tuple(gots), kepts))
    places = [place_in(gots, piece.got) for piece in arrived]
    for piece, place in zip(arrived, places):
        piece.got = tied[1][place]
    for piece, kept in zip(ready, tied[2]):
        piece.kept = kept
    return tied[0]


def split_rows(total, core, rows_each):
    rows, columns = total.shape
    cut = total.reshape(rows // (2 * rows_each), 2, rows_each, columns)
    first, second = cut[:, 0], cut[:, 1]
    even = core == 0
    return jnp.where(even, second, first).astype(bf16), jnp.where(even, first, second).astype(bf16)


def panels_of(blocks, panels, rows_each):
    spec = pl.BlockSpec((blocks, None, rows_each, LANES), lambda i: (0, i, 0, 0))
    return spec, jax.ShapeDtypeStruct((blocks, panels, rows_each, LANES), bf16)


def row_stats(values):
    mean = jnp.mean(values, axis=-1, keepdims=True)
    centred = values - mean
    scale = lax.rsqrt(jnp.mean(centred * centred, axis=-1, keepdims=True) + epsilon)
    return centred * scale, scale


def norm_back(values, gain, grad):
    normal, scale = row_stats(values)
    inner = grad * gain
    along = jnp.mean(inner * normal, axis=-1, keepdims=True)
    return scale * (inner - jnp.mean(inner, axis=-1, keepdims=True) - normal * along), grad * normal


def add_rows(out_ref, *each):
    @pl.when(pl.program_id(0) == 0)
    def _():
        out_ref[...] = jnp.zeros_like(out_ref)

    for row, values in enumerate(each):
        out_ref[row : row + 1, :] += jnp.sum(values, axis=0, keepdims=True)


def enter_kernel(part, mirror, merge, gain, shift, qkv, *rest):
    hidden, normed, projected = rest[-3:]
    value = part[...] + nn(mirror[...], merge[...])
    hidden[...] = value
    low = (row_stats(value)[0] * gain[...] + shift[...]).astype(bf16)
    normed[...] = low
    projected[...] = nn(low, qkv[...]).astype(bf16)


def enter(start, part, mirror, merge_low, gain, shift, qkv, before):
    tokens = part.shape[0]
    offset = start // TILE
    at = lambda columns: pl.BlockSpec((TILE, columns), lambda i: (offset + i, 0))
    operands = (part, mirror, merge_low, gain, shift, qkv)
    return pl.pallas_call(
        enter_kernel,
        grid=(mirror.shape[0] // TILE,),
        in_specs=[at(D), tiled(D), held((D, D)), held((1, D)), held((1, D)), held((D, 3 * D))]
        + [pl.BlockSpec(memory_space=pl.ANY)] * len(before),
        out_specs=[at(D), at(D), at(3 * D)],
        out_shape=[
            jax.ShapeDtypeStruct((tokens, D), f32),
            jax.ShapeDtypeStruct((tokens, D), bf16),
            jax.ShapeDtypeStruct((tokens, 3 * D), bf16),
        ],
        input_output_aliases={len(operands) + i: i for i in range(len(before))},
        compiler_params=settings(),
        cost_estimate=cost(8 * mirror.shape[0] * D * D, 26 * MIB),
        name="enter",
    )(*operands, *before)


def leave_kernel(hidden, mixed, out_weight, gain, shift, residual, normed):
    value = hidden[...] + nn(mixed[...], out_weight[...])
    residual[...] = value
    normed[...] = (row_stats(value)[0] * gain[...] + shift[...]).astype(bf16)


def leave(hidden, mixed, out_weight, gain, shift):
    tokens = hidden.shape[0]
    return pl.pallas_call(
        leave_kernel,
        grid=(tokens // TILE,),
        in_specs=[tiled(D), tiled(D), held((D, D)), held((1, D)), held((1, D))],
        out_specs=[tiled(D), tiled(D)],
        out_shape=[jax.ShapeDtypeStruct((tokens, D), f32), jax.ShapeDtypeStruct((tokens, D), bf16)],
        compiler_params=settings(),
        cost_estimate=cost(2 * tokens * D * D, 14 * MIB),
        name="leave",
    )(hidden, mixed, out_weight, gain, shift)


def windows(lengths):
    ends = jnp.cumsum(lengths, axis=1)
    starts = ends - lengths
    low = (jnp.arange(BLOCKS, dtype=jnp.int32) * BLOCK)[None, :, None]
    holds_low = (low >= starts[:, None, :]) & (low < ends[:, None, :])
    high = low + (BLOCK - 1)
    holds_high = (high >= starts[:, None, :]) & (high < ends[:, None, :])
    window_low = jnp.sum(jnp.where(holds_low, starts[:, None, :], 0), axis=2) // BLOCK
    window_high = (jnp.sum(jnp.where(holds_high, ends[:, None, :], 0), axis=2) + BLOCK - 1) // BLOCK
    return window_low.reshape(-1), (window_high - window_low).reshape(-1)


def row_segments(lengths):
    ends = jnp.cumsum(lengths, axis=1)
    position = jnp.arange(ROW_LEN, dtype=jnp.int32)
    return jnp.sum((position[None, :, None] >= ends[:, None, :]).astype(jnp.int32), axis=2)


def head_slopes():
    return jnp.array([2.0 ** (-8.0 * (head + 1.0) / H) for head in range(H)], f32)


def fill_distance(far_ref, column, line):
    for b in range(BLOCKS):
        rows = slice(b * BLOCK, (b + 1) * BLOCK)
        i = lax.broadcasted_iota(jnp.int32, (BLOCK, ROW_LEN), 0) + b * BLOCK
        j = lax.broadcasted_iota(jnp.int32, (BLOCK, ROW_LEN), 1)
        distance = jnp.abs(i - j).astype(f32)
        far_ref[rows, :] = jnp.where(column[rows, :] == line[...], distance, FAR)


def masked_pair(value, lows):
    zero = jnp.zeros_like(value)
    return jnp.concatenate([jnp.where(lows, value, zero), jnp.where(lows, zero, value)], axis=0)


def over_blocks(low_ref, count_ref, row, variant):
    def block(b, carry):
        rows = pl.ds(pl.multiple_of(b * BLOCK, BLOCK), BLOCK)
        start = pl.multiple_of(low_ref[row * BLOCKS + b] * BLOCK, BLOCK)
        count = count_ref[row * BLOCKS + b]
        for n in range(1, BLOCKS + 1):
            pl.when(count == n)(functools.partial(variant, rows, pl.ds(start, n * BLOCK)))
        return carry

    lax.fori_loop(0, BLOCKS, block, 0)


def attend_kernel(
    low_ref, count_ref, slope_ref, column, line, q_ref, k_ref, v_ref, o_ref, lse_ref, far_ref, value_ref
):
    row = pl.program_id(0)
    group = pl.program_id(1)

    @pl.when(group == 0)
    def _():
        fill_distance(far_ref, column, line)
        lse_ref[...] = jnp.zeros_like(lse_ref)

    lane = lax.broadcasted_iota(jnp.int32, (1, 128), 1)
    lows = lane < HD
    for pair in range(HEADS // 2):
        value_ref[pair, :, :128] = v_ref[:, pair * 128 : pair * 128 + 128]
        value_ref[pair, :, 128:] = jnp.ones((ROW_LEN, 128), bf16)

    def variant(rows, cols):
        far = far_ref[rows, cols]
        logs = lse_ref[rows, :]
        for pair in range(HEADS // 2):
            at = slice(pair * 128, pair * 128 + 128)
            head = group * HEADS + pair * 2
            query = masked_pair(q_ref[rows, at] * bf16(HD**-0.5), lows)
            score = nt(query, k_ref[cols, at])
            score = score - jnp.concatenate([slope_ref[head] * far, slope_ref[head + 1] * far], axis=0)
            top = jnp.max(score, axis=1, keepdims=True)
            soft = jnp.exp(score - top).astype(bf16)
            both = nn(soft, value_ref[pair, cols, :])
            total = both[:, 128:]
            log_total = top + jnp.log(total)
            logs = jnp.where(lane == head, log_total[:BLOCK], logs)
            logs = jnp.where(lane == head + 1, log_total[BLOCK:], logs)
            mixed = jnp.where(lows, both[:BLOCK, :128], both[BLOCK:, :128])
            o_ref[rows, at] = (mixed / jnp.where(lows, total[:BLOCK], total[BLOCK:])).astype(bf16)
        lse_ref[rows, :] = logs

    over_blocks(low_ref, count_ref, row, variant)


def head_group(part):
    return pl.BlockSpec((ROW_LEN, HEADS * HD), lambda r, g, *_: (r, part * GROUPS + g))


def attention_operands(lengths):
    rows = lengths.shape[0]
    segments = row_segments(lengths)
    return windows(lengths) + (
        head_slopes(),
        segments.reshape(rows * ROW_LEN, 1),
        segments.reshape(rows, 1, ROW_LEN),
    )


def segment_specs():
    return [
        pl.BlockSpec((ROW_LEN, 1), lambda r, *_: (r, 0)),
        pl.BlockSpec((None, 1, ROW_LEN), lambda r, *_: (r, 0, 0)),
    ]


def attend(projected, operands):
    tokens = projected.shape[0]
    rows = tokens // ROW_LEN
    return launch(
        attend_kernel,
        operands + (projected, projected, projected),
        scalars=3,
        out_shape=[jax.ShapeDtypeStruct((tokens, D), bf16), jax.ShapeDtypeStruct((tokens, 128), f32)],
        grid=(rows, GROUPS),
        in_specs=segment_specs() + [head_group(0), head_group(1), head_group(2)],
        out_specs=[head_group(0), pl.BlockSpec((ROW_LEN, 128), lambda r, g, *_: (r, 0))],
        scratch_shapes=[
            pltpu.VMEM((ROW_LEN, ROW_LEN), f32),
            pltpu.VMEM((HEADS // 2, ROW_LEN, 256), bf16),
        ],
        compiler_params=settings(),
        cost_estimate=cost(rows * 20e9, 30 * MIB),
        name="attend",
    )


def attend_back_kernel(
    group,
    low_ref,
    count_ref,
    slope_ref,
    column,
    line,
    q_ref,
    k_ref,
    v_ref,
    grad_ref,
    lse_ref,
    delta_ref,
    out_ref,
    far_ref,
    turned_ref,
    key_ref,
):
    row = pl.program_id(0)
    fill_distance(far_ref, column, line)
    lows = lax.broadcasted_iota(jnp.int32, (1, 128), 1) < HD
    tops = lax.broadcasted_iota(jnp.int32, (128, 1), 0) < HD
    turned_ref[...] = jnp.zeros_like(turned_ref)
    for pair in range(HEADS // 2):
        key_ref[pair] = k_ref[:, pair * 128 : pair * 128 + 128].T

    def variant(rows, cols):
        far = far_ref[rows, cols]
        for pair in range(HEADS // 2):
            at = slice(pair * 128, pair * 128 + 128)
            head = group * HEADS + pair * 2
            query = q_ref[cols, at] * bf16(HD**-0.5)
            grad = grad_ref[cols, at]
            score = nt(masked_pair(k_ref[rows, at], lows), query)
            soft_grad = nt(masked_pair(v_ref[rows, at], lows), grad)
            softs, score_grads = [], []
            for side in range(2):
                part = slice(side * BLOCK, side * BLOCK + BLOCK)
                own = pl.ds(pair * 2 + side, 1)
                soft = jnp.exp(score[part] - slope_ref[head + side] * far - lse_ref[own, cols])
                score_grads.append((soft * (soft_grad[part] - delta_ref[own, cols])).astype(bf16))
                softs.append(soft.astype(bf16))
            score_grad = jnp.concatenate(score_grads, axis=0)
            value_grad = nn(jnp.concatenate(softs, axis=0), grad)
            key_grad = nn(score_grad, query)
            out_ref[2, rows, at] = jnp.where(lows, value_grad[:BLOCK], value_grad[BLOCK:]).astype(bf16)
            out_ref[1, rows, at] = jnp.where(lows, key_grad[:BLOCK], key_grad[BLOCK:]).astype(bf16)
            key = key_ref[pair, :, rows]
            zero = jnp.zeros_like(key)
            keys = jnp.concatenate([jnp.where(tops, key, zero), jnp.where(tops, zero, key)], axis=1)
            turned_ref[at, cols] += nn(keys, score_grad)

    over_blocks(low_ref, count_ref, row, variant)
    out_ref[0] = (turned_ref[...].T * HD**-0.5).astype(bf16)


def attend_back(group, projected, grad, lse_rows, delta_rows, operands, pins):
    tokens = projected.shape[0]
    rows = tokens // ROW_LEN
    of_group = lambda part: pl.BlockSpec((ROW_LEN, HEADS * HD), lambda r, *_: (r, part * GROUPS + group))
    thin = pl.BlockSpec((None, HEADS, ROW_LEN), lambda r, *_: (r, group, 0))
    return launch(
        functools.partial(attend_back_kernel, group),
        operands + (projected, projected, projected, grad, lse_rows, delta_rows),
        pins,
        scalars=3,
        out_shape=jax.ShapeDtypeStruct((3, tokens, HEADS * HD), bf16),
        grid=(rows,),
        in_specs=segment_specs() + [of_group(0), of_group(1), of_group(2), of_group(0), thin, thin],
        out_specs=pl.BlockSpec((3, ROW_LEN, HEADS * HD), lambda r, *_: (0, r, 0)),
        scratch_shapes=[
            pltpu.VMEM((ROW_LEN, ROW_LEN), f32),
            pltpu.VMEM((HEADS * HD, ROW_LEN), f32),
            pltpu.VMEM((HEADS // 2, 128, ROW_LEN), bf16),
        ],
        compiler_params=settings(),
        cost_estimate=cost(rows * 18e9, 16 * MIB),
        name="attend_back",
    )


PULL = 0.44
ERFC = (
    0.1241083994,
    0.1244657618,
    0.1084788423,
    0.1084610390,
    -0.0110834557,
    0.1493682951,
    -0.1395405297,
    0.0357417408,
)


def gelu_pair(value):
    size = jnp.abs(value)
    t = 1.0 / (1.0 + (PULL * 0.5**0.5) * size)
    poly = jnp.full_like(t, ERFC[-1])
    for term in reversed(ERFC[:-1]):
        poly = poly * t + term
    bell = jnp.exp(value * value * -0.5)
    tail = bell * t * poly
    whole = jnp.where(value < 0, tail, 1.0 - tail)
    return value * whole, whole + value * (bell * (0.5 / jnp.pi) ** 0.5)


def feed_kernel(
    rows_up,
    rows_down,
    core_ref,
    normed,
    cotangent,
    up_weight,
    up_bias,
    back,
    activated,
    normed_grad,
    bias_grad,
    up_sent,
    up_kept,
    down_sent,
    down_kept,
):
    core = core_ref[0]

    @pl.when(pl.program_id(0) == 0)
    def _():
        normed_grad[...] = jnp.zeros_like(normed_grad)

    value = nn(normed[...], up_weight[...]) + up_bias[...]
    active, slope = gelu_pair(value)
    active = active.astype(bf16)
    activated[...] = active
    grad = (back[...].astype(f32) * slope).astype(bf16)
    bias_grad[...] = jnp.sum(grad.astype(f32), axis=0, keepdims=True)
    normed_grad[...] += nt(grad, up_weight[...])
    for value, out in zip(split_rows(tn(active, cotangent[...]), core, rows_down), (down_sent, down_kept)):
        for panel in range(D // LANES):
            out[:, panel] = value[:, :, panel * LANES : panel * LANES + LANES]
    up_sent[...], up_kept[...] = split_rows(tn(normed[...], grad), core, rows_up)


def feed(core, normed, cotangent, up_weight, up_bias, back, width=LANES):
    tokens = normed.shape[0]
    hidden_units = up_weight.shape[1]
    devices = lax.axis_size("half") * lax.axis_size("dp")
    across = lambda rows: pl.BlockSpec((rows, width), lambda i: (0, i))
    shape = jax.ShapeDtypeStruct
    up_spec, up_shape = panels_of(devices // 2, hidden_units // LANES, D // devices)
    rows_down = hidden_units // devices
    down_spec = pl.BlockSpec((width // (2 * rows_down), D // LANES, rows_down, LANES), lambda i: (i, 0, 0, 0))
    down_shape = shape((devices // 2, D // LANES, rows_down, LANES), bf16)
    return launch(
        functools.partial(feed_kernel, D // devices, hidden_units // devices),
        (core, normed, cotangent, up_weight, up_bias, back),
        grid=(hidden_units // width,),
        in_specs=[
            pl.BlockSpec(memory_space=pltpu.SMEM),
            held((tokens, D)),
            held((tokens, D)),
            across(D),
            across(1),
            across(tokens),
        ],
        out_specs=[
            across(tokens),
            pl.BlockSpec((tokens, D), lambda i: (0, 0)),
            across(1),
            up_spec,
            up_spec,
            down_spec,
            down_spec,
        ],
        out_shape=[
            shape((tokens, hidden_units), bf16),
            shape((tokens, D), f32),
            shape((1, hidden_units), f32),
            up_shape,
            up_shape,
            down_shape,
            down_shape,
        ],
        compiler_params=settings(),
        cost_estimate=cost(8 * tokens * D * hidden_units, 60 * MIB),
        name="feed",
    )


def output_kernel(activated, down_weight, residual, bias, output):
    output[...] = (residual[...] + bias[...] + nn(activated[...], down_weight[...])).astype(bf16)


def layer_output(activated, down_weight, residual, bias, pins):
    tokens, hidden_units = activated.shape
    across = lambda rows: pl.BlockSpec((rows, TILE), lambda i: (0, i))
    return launch(
        output_kernel,
        (activated, down_weight, residual, bias),
        pins,
        grid=(D // TILE,),
        in_specs=[held((tokens, hidden_units)), across(hidden_units), across(tokens), across(1)],
        out_specs=across(tokens),
        out_shape=jax.ShapeDtypeStruct((tokens, D), bf16),
        compiler_params=settings(),
        cost_estimate=cost(2 * tokens * D * hidden_units, 24 * MIB),
        name="layer_output",
    )


def second_back_kernel(
    normed_grad,
    residual,
    cotangent,
    gain,
    out_weight,
    mixed,
    lse,
    residual_grad,
    attention_grad,
    mixed_grad,
    delta_rows,
    lse_rows,
    sums,
):
    incoming = normed_grad[...]
    outer = cotangent[...].astype(f32)
    through, gain_terms = norm_back(residual[...], gain[...], incoming)
    value = outer + through
    residual_grad[...] = value
    low = value.astype(bf16)
    attention_grad[...] = low
    mixed_low = nt(low, out_weight[...]).astype(bf16)
    mixed_grad[...] = mixed_low
    product = mixed_low.astype(f32) * mixed[...].astype(f32)
    high = product.astype(bf16)
    rest = (product - high.astype(f32)).astype(bf16)
    of_head = lax.broadcasted_iota(jnp.int32, (H, D), 1) // HD
    member = (of_head == lax.broadcasted_iota(jnp.int32, (H, D), 0)).astype(bf16)
    delta_rows[...] = nt(member, high) + nt(member, rest)
    lse_rows[...] = lse[...].T[:H]
    add_rows(sums, gain_terms, incoming, outer)


def second_back(normed_grad, residual, cotangent, gain, out_weight, mixed, lse):
    tokens = residual.shape[0]
    per_row = ROW_LEN // TILE
    shape = jax.ShapeDtypeStruct
    thin = pl.BlockSpec((None, H, TILE), lambda i: (i // per_row, 0, i % per_row))
    return pl.pallas_call(
        second_back_kernel,
        grid=(tokens // TILE,),
        in_specs=[tiled(D), tiled(D), tiled(D), held((1, D)), held((D, D)), tiled(D), tiled(128)],
        out_specs=[tiled(D), tiled(D), tiled(D), thin, thin, summed_over(D)],
        out_shape=[
            shape((tokens, D), f32),
            shape((tokens, D), bf16),
            shape((tokens, D), bf16),
            shape((tokens // ROW_LEN, H, ROW_LEN), f32),
            shape((tokens // ROW_LEN, H, ROW_LEN), f32),
            shape((8, D), f32),
        ],
        compiler_params=settings(),
        cost_estimate=cost(3 * tokens * D * D, 22 * MIB),
        name="second_back",
    )(normed_grad, residual, cotangent, gain, out_weight, mixed, lse)


def first_back_kernel(
    first, second, hidden, residual_grad, gain, qkv, hidden_grad, sums
):
    incoming = jnp.zeros(hidden.shape, f32)
    wide = HEADS * HD
    for part in range(3):
        for at, grad in enumerate((first, second)):
            start = part * D + at * wide
            incoming += nt(grad[part], qkv[:, start : start + wide])
    through, gain_terms = norm_back(hidden[...], gain[...], incoming)
    low = (residual_grad[...] + through).astype(bf16)
    hidden_grad[...] = low
    add_rows(sums, gain_terms, incoming, low.astype(f32))


def first_back(projected_grads, hidden, residual_grad, gain, qkv, pins):
    tokens = hidden.shape[0]
    shape = jax.ShapeDtypeStruct
    group = pl.BlockSpec((3, TILE, HEADS * HD), lambda i: (0, i, 0))
    return launch(
        first_back_kernel,
        projected_grads + (hidden, residual_grad, gain, qkv),
        pins,
        grid=(tokens // TILE,),
        in_specs=[group, group, tiled(D), tiled(D), held((1, D)), held((D, 3 * D))],
        out_specs=[tiled(D), summed_over(D)],
        out_shape=[shape((tokens, D), bf16), shape((8, D), f32)],
        compiler_params=settings(),
        cost_estimate=cost(6 * tokens * D * D, 22 * MIB),
        name="first_back",
    )


def joined_kernel(grad, merge, out):
    out[...] = nt(grad[...], merge[...]).astype(bf16)


def joined_grad(hidden_grad, merge_half, pins, name):
    tokens = hidden_grad.shape[0]
    return launch(
        joined_kernel,
        (hidden_grad, merge_half),
        pins,
        grid=(tokens // TILE,),
        in_specs=[tiled(D), held((D, D))],
        out_specs=tiled(D),
        out_shape=jax.ShapeDtypeStruct((tokens, D), bf16),
        compiler_params=settings(),
        cost_estimate=cost(2 * tokens * D * D, 6 * MIB),
        name=name,
    )


def weight_kernel(rows_each, core_ref, left, right, sent, kept):
    sent[...], kept[...] = split_rows(tn(left[...], right[...]), core_ref[0], rows_each)


def out_query_kernel(rows_each, core_ref, mixed, attention_grad, normed, projected_grad, sent, kept):
    step = pl.program_id(0)
    first = D // (HEADS * HD)

    @pl.when(step < first)
    def _():
        weight_kernel(rows_each, core_ref, mixed, attention_grad, sent, kept)

    @pl.when(step >= first)
    def _():
        weight_kernel(rows_each, core_ref, normed, projected_grad, sent, kept)


def out_query_grad(core, mixed, attention_grad, normed, projected_grad, pins):
    tokens = mixed.shape[0]
    devices = lax.axis_size("half") * lax.axis_size("dp")
    width = HEADS * HD
    first = D // width
    out, out_shape = panels_of(devices // 2, first + 3, D // devices)
    return launch(
        functools.partial(out_query_kernel, D // devices),
        (core, mixed, attention_grad, normed, projected_grad),
        pins,
        grid=(first + 3,),
        in_specs=[
            pl.BlockSpec(memory_space=pltpu.SMEM),
            held((tokens, D)),
            pl.BlockSpec((tokens, width), lambda i: (0, jnp.minimum(i, first - 1))),
            held((tokens, D)),
            pl.BlockSpec((None, tokens, width), lambda i: (jnp.maximum(i - first, 0), 0, 0)),
        ],
        out_specs=[out, out],
        out_shape=[out_shape, out_shape],
        compiler_params=settings(),
        cost_estimate=cost(2 * tokens * D * (first + 3) * width, 20 * MIB),
        name="out_query_grad",
    )


def merge_kernel(rows_each, core_ref, frames, *refs):
    mirrors, (right, sent, kept) = refs[:-3], refs[-3:]
    half = sent.shape[0] // 2
    sent[:half], kept[:half] = split_rows(tn(frames[...], right[...]), core_ref[0], rows_each)
    total = jnp.zeros((D, right.shape[1]), f32)
    start = 0
    for mirror in mirrors:
        end = start + mirror.shape[0]
        total += tn(mirror[...], right[start:end, :])
        start = end
    sent[half:], kept[half:] = split_rows(total, core_ref[0], rows_each)


def merge_grad(core, frames, mirrors, right, width=LANES):
    tokens = frames.shape[0]
    devices = lax.axis_size("half") * lax.axis_size("dp")
    out, out_shape = panels_of(devices // 2, D // width, 2 * D // devices)
    return launch(
        functools.partial(merge_kernel, 2 * D // devices),
        (core, frames, *mirrors, right),
        grid=(D // width,),
        in_specs=[pl.BlockSpec(memory_space=pltpu.SMEM), held((tokens, D))]
        + [held(mirror.shape) for mirror in mirrors]
        + [pl.BlockSpec((tokens, width), lambda i: (0, i))],
        out_specs=[out, out],
        out_shape=[out_shape, out_shape],
        compiler_params=settings(),
        cost_estimate=cost(4 * tokens * D * D, 16 * MIB),
        name="merge_grad",
    )


def query_grad(core, normed, projected_grad):
    tokens = normed.shape[0]
    devices = lax.axis_size("half") * lax.axis_size("dp")
    width = HEADS * HD
    out, out_shape = panels_of(devices // 2, 3, D // devices)
    return launch(
        functools.partial(weight_kernel, D // devices),
        (core, normed, projected_grad),
        grid=(3,),
        in_specs=[
            pl.BlockSpec(memory_space=pltpu.SMEM),
            held((tokens, D)),
            pl.BlockSpec((None, tokens, width), lambda i: (i, 0, 0)),
        ],
        out_specs=[out, out],
        out_shape=[out_shape, out_shape],
        compiler_params=settings(),
        cost_estimate=cost(6 * tokens * D * width, 16 * MIB),
        name="query_grad",
    )


def on_device(
    frames,
    skip_rows,
    lengths,
    merge_weight,
    merge_bias,
    norm1_gain,
    norm1_bias,
    qkv_weight,
    out_weight,
    norm2_gain,
    norm2_bias,
    up_weight,
    up_bias,
    down_weight,
    down_bias,
    cotangent,
):
    tokens = frames.shape[0]
    line = lambda vector: vector.reshape(1, -1)
    core = (lax.axis_index("dp") & 1).astype(jnp.int32).reshape(1)
    mirrors = [swapped(skip_rows[start:end], "half", 0) for start, end in zip(CUTS[:-1], CUTS[1:])]
    operands = attention_operands(lengths)
    back = nt(cotangent, down_weight).astype(bf16)
    part = nn(frames, merge_weight[:D]) + merge_bias
    entered = ()
    for start, mirror in zip(CUTS, mirrors):
        entered = enter(
            start, part, mirror, merge_weight[D:], line(norm1_gain), line(norm1_bias), qkv_weight, entered
        )
    hidden, normed, projected = entered
    mixed, lse = attend(projected, operands)
    residual, normed_two = leave(hidden, mixed, out_weight, line(norm2_gain), line(norm2_bias))
    activated, normed_two_grad, up_bias_grad, up_sent, up_kept, down_sent, down_kept = feed(
        core, normed_two, cotangent, up_weight, line(up_bias), back
    )
    _, x, y, (l, *deep) = digits()
    down = started(down_sent, down_kept)
    up = started(up_sent, up_kept)
    residual_grad, attention_grad, mixed_grad, delta_rows, lse_rows, sums_two = second_back(
        normed_two_grad, residual, cotangent, line(norm2_gain), out_weight, mixed, lse
    )
    (mixed_grad,) = in_order((mixed_grad,), (down,))
    cut = down.rows // 2
    one, two = mix([(down, ((0, cut, x), (cut, down.rows, y)))])
    (mixed_grad,) = in_order((mixed_grad,), (up,), (one, two))
    cut = up.rows // 2
    three, = mix([(up, ((0, cut, l),))])
    four = (cut, up.rows)
    (mixed_grad,) = in_order((mixed_grad,), (), (three,))
    first = attend_back(0, projected, mixed_grad, lse_rows, delta_rows, operands, ())
    (first,) = in_order((first,), (one, two, three))
    one, two, three, four = mix([(one, cuts(one, y)), (two, cuts(two, l)), (three, cuts(three, x)), (up, ((*four, x),))])
    (first,) = in_order((first,), (), (one, two, three, four))
    out_query = started(*out_query_grad(core, mixed, attention_grad, normed, first, ()))
    (mixed_grad,) = in_order((mixed_grad,), (), (out_query,))
    second = attend_back(1, projected, mixed_grad, lse_rows, delta_rows, operands, ())
    (second,) = in_order((second,), (one, two, three, four, out_query))
    panel = D // (lax.axis_size("half") * lax.axis_size("dp"))
    cut = 3 * panel
    one, two, three, four, out_one, out_two = mix(
        [
            (one, cuts(one, l)),
            (two, cuts(two, x)),
            (three, cuts(three, y)),
            (four, cuts(four, y)),
            (out_query, ((0, cut, x), (cut, out_query.rows, l))),
        ]
    )
    (second,) = in_order((second,), (), (one, two, three, four, out_one, out_two))
    query = started(*query_grad(core, normed, second))
    (second,) = in_order((second,), (), (query,))
    hidden_grad, sums_one = first_back(
        (first, second), hidden, residual_grad, line(norm1_gain), qkv_weight, ()
    )
    skip_parts = [
        joined_grad(hidden_grad[start:end], merge_weight[D:], (), "skip_grad")
        for start, end in zip(SKIP_CUTS[:-1], SKIP_CUTS[1:])
    ]
    (hidden_grad, sums_one, *skip_parts) = in_order(
        (hidden_grad, sums_one, *skip_parts), (one, two, three, four, out_one, out_two, query)
    )
    skip_one = Sent(skip_parts[0], "half", 0)
    one, two, three, four, out_one, out_two, query = mix(
        [
            (one, cuts(one, deep[0])),
            (two, cuts(two, deep[0])),
            (three, cuts(three, deep[0])),
            (four, cuts(four, l)),
            (out_one, cuts(out_one, y)),
            (out_two, cuts(out_two, y)),
            (query, cuts(query, l)),
        ]
    )
    (hidden_grad,) = in_order((hidden_grad,), (), (one, two, three, four, out_one, out_two, query))
    vectors = vector_piece((sums_one[2], sums_one[0], sums_one[1], sums_two[0], sums_two[1], up_bias_grad, sums_two[2]))
    merge = started(*merge_grad(core, frames, mirrors, hidden_grad))
    (hidden_grad,) = in_order((hidden_grad,), (), (merge,))
    frames_grad = joined_grad(hidden_grad, merge_weight[:D], (), "frames_grad")
    (frames_grad, residual, skip_parts[1]) = in_order(
        (frames_grad, residual, skip_parts[1]),
        (merge, vectors, skip_one, one, two, three, four, out_one, out_two, query),
    )
    skip_two = Sent(skip_parts[1], "half", 0)
    cut = merge.rows // 2
    done = [one, two, three]
    four, out_one, out_two, query, merge_one, merge_two, vectors = mix(
        [
            (four, cuts(four, deep[0])),
            (out_one, cuts(out_one, l)),
            (out_two, cuts(out_two, deep[0])),
            (query, cuts(query, y)),
            (merge, ((0, cut, y), (cut, merge.rows, l))),
            (vectors, cuts(vectors, y)),
        ]
    )
    (residual,) = in_order((residual,), (), (four, out_one, out_two, query, merge_one, merge_two, vectors))
    output = layer_output(activated, down_weight, residual, line(down_bias), ())
    (output,) = in_order((output,), (four, out_one, out_two, query, merge_one, merge_two, vectors))
    out_one, out_two, query, merge_one, merge_two, vectors = mix(
        [
            (out_one, cuts(out_one, deep[0])),
            (out_two, cuts(out_two, x)),
            (query, cuts(query, deep[0])),
            (merge_one, cuts(merge_one, l)),
            (merge_two, cuts(merge_two, y)),
            (vectors, cuts(vectors, l)),
        ]
    )
    query, merge_one, merge_two, vectors = mix(
        [
            (query, cuts(query, x)),
            (merge_one, cuts(merge_one, deep[0])),
            (merge_two, cuts(merge_two, deep[0])),
            (vectors, cuts(vectors, deep[0])),
        ]
    )
    merge_one, merge_two, vectors = mix([(each, cuts(each, x)) for each in (merge_one, merge_two, vectors)])
    pieces = [one, two, three, four, out_one, out_two, query, merge_one, merge_two, vectors]
    while any(piece.left for piece in pieces):
        open_pieces = [piece for piece in pieces if piece.left]
        closed = mix([(piece, cuts(piece, piece.left[0])) for piece in open_pieces])
        pieces = [closed.pop(0) if piece.left else piece for piece in pieces]
    one, two, three, four, out_one, out_two, query, merge_one, merge_two, vectors = pieces
    devices = lax.axis_size("half") * lax.axis_size("dp")
    hidden_units = up_weight.shape[1]
    wide = HEADS * HD
    per = three.rows // panel
    plan = [(one, 0, 0, 0), (two, 0, 0, LANES)]
    plan += [(three, at * panel, 1, at * LANES) for at in range(per)]
    plan += [(four, at * panel, 1, (per + at) * LANES) for at in range(per)]
    plan += [(out_one, 0, 2, 0), (out_one, panel, 2, LANES), (out_one, 2 * panel, 3, 0)]
    plan += [(out_two, at * panel, 3, (at + 1) * D) for at in range(2)]
    plan += [(query, at * panel, 3, at * D + wide) for at in range(3)]
    plan += [(merge_one, 0, 4, 0), (merge_two, 0, 4, LANES), (vectors, 0, 5, 0)]
    down_weight_grad, up_weight_grad, out_weight_grad, qkv_weight_grad, merge_weight_grad, sums = finish(
        [
            (hidden_units // devices, D),
            (D // devices, hidden_units),
            (D // devices, D),
            (D // devices, 3 * D),
            (2 * D // devices, D),
            (VECTOR_ROWS, LANES),
        ],
        plan,
    )
    small = []
    start = 0
    for size in (D, D, D, D, D, hidden_units, D):
        small.append(sums[0, start : start + size // devices])
        start += size // devices
    skip_grad = jnp.concatenate((skip_one.got, skip_two.got), axis=0)
    return (
        output,
        frames_grad,
        skip_grad,
        merge_weight_grad,
        small[0],
        small[1],
        small[2],
        qkv_weight_grad,
        out_weight_grad,
        small[3],
        small[4],
        up_weight_grad,
        small[5],
        down_weight_grad,
        small[6],
    )


def cuts(piece, digit):
    return ((0, piece.rows, digit),)


def solution(mesh):
    rows = P(("half", "dp"), None)
    parts = P(("half", "dp"))
    in_specs = (rows, rows, rows) + (P(),) * 12 + (rows,)
    out_specs = (rows, rows, rows, rows, parts, parts, parts, rows, rows, parts, parts, rows, parts, rows, parts)
    return jax.shard_map(
        on_device, mesh=mesh, in_specs=in_specs, out_specs=out_specs, check_vma=False
    )
```

```python
import functools

import jax
import jax.numpy as jnp
from jax import lax
from jax.experimental import pallas as pl
from jax.experimental.pallas import tpu as pltpu
from jax.sharding import PartitionSpec as P

D = 1024
H = 16
HD = 64
ROW_LEN = 1024
BLOCK = 128
BLOCKS = ROW_LEN // BLOCK
TILE = 256
CUTS = (0, 768, 1024)
LANES = 512
VECTOR_ROWS = 16
HEADS = 8
GROUPS = H // HEADS
FAR = 1e30
epsilon = 1e-05
f32 = jnp.float32
bf16 = jnp.bfloat16
MIB = 1024 * 1024


def nn(left, right):
    return jnp.dot(left, right, preferred_element_type=f32)


def nt(left, right):
    return lax.dot_general(left, right, (((1,), (1,)), ((), ())), preferred_element_type=f32)


def tn(left, right):
    return lax.dot_general(left, right, (((0,), (0,)), ((), ())), preferred_element_type=f32)


def settings(megabytes):
    return pltpu.CompilerParams(vmem_limit_bytes=megabytes * MIB)


def cost(flops, moved):
    return pl.CostEstimate(flops=int(flops), bytes_accessed=int(moved), transcendentals=0)


def held(shape):
    zeros = (0,) * len(shape)
    return pl.BlockSpec(shape, lambda *_: zeros, pipeline_mode=pl.Buffered(1))


def tiled(columns):
    return pl.BlockSpec((TILE, columns), lambda i: (i, 0))


def summed_over(columns):
    return pl.BlockSpec((8, columns), lambda i: (0, 0))


def launch(kernel, operands, pins=(), in_specs=(), scalars=0, **rest):
    count, extra = len(operands), len(pins)

    def body(*refs):
        kernel(*refs[:count], *refs[count + extra :])

    in_specs = list(in_specs) + [pl.BlockSpec(memory_space=pl.ANY)] * extra
    if scalars:
        rest["grid_spec"] = pltpu.PrefetchScalarGridSpec(
            num_scalar_prefetch=scalars,
            grid=rest.pop("grid"),
            in_specs=in_specs,
            out_specs=rest.pop("out_specs"),
            scratch_shapes=rest.pop("scratch_shapes"),
        )
    else:
        rest["in_specs"] = in_specs
    return pl.pallas_call(body, **rest)(*operands, *pins)


def swapped(value, axis, apart):
    mask = 2**apart
    pairs = [(source, source ^ mask) for source in range(lax.axis_size(axis))]
    return lax.ppermute(value, axis, pairs)


def mesh_bits():
    dp_bits = lax.axis_size("dp").bit_length() - 1
    half_bits = lax.axis_size("half").bit_length() - 1
    return [("half", bit) for bit in reversed(range(half_bits))] + [
        ("dp", bit) for bit in reversed(range(dp_bits))
    ]


def digits():
    count = len(mesh_bits())
    return count - 1, 0, count - 2, list(range(count - 3, 0, -1))


def my_sides():
    return jnp.stack([(lax.axis_index(axis) >> apart) & 1 for axis, apart in mesh_bits()]).astype(jnp.int32)


class Piece:
    def __init__(self, left, rows, kept, got=None, offset=0):
        self.left, self.rows, self.kept, self.got, self.offset = tuple(left), rows, kept, got, offset


def started(sent, kept):
    count = len(mesh_bits()) - 1
    flat = lambda value: value.reshape(-1, LANES)
    kept = flat(kept)
    return Piece(range(count), kept.shape[0] >> count, kept, swapped(flat(sent), "dp", 0))


def mix_kernel(plan, loaded, sides_ref, *refs):
    for take in plan:
        low, rows = take["bits"], take["rows"]
        for to, offset, other in ((take["to_sent"], take["sent_at"], True), (take["to_kept"], 0, False)):
            if to is None:
                continue
            out = refs[loaded + to]
            side = None
            if take["digit"] is not None:
                side = sides_ref[take["digit"]]
                side = 1 - side if other else side

            def one(at, carry, side=side, out=out, offset=offset, take=take, low=low, rows=rows):
                block = at if side is None else ((((at >> low) * 2) + side) << low) + (at & ((1 << low) - 1))
                start = block * take["whole"] + take["first"]
                total = refs[take["kept"]][pl.ds(pl.multiple_of(start, 8), rows), :]
                if take["got"] is not None:
                    theirs = refs[take["got"]][pl.ds(pl.multiple_of(take["got_at"] + start, 8), rows), :]
                    total = (total.astype(f32) + theirs.astype(f32)).astype(bf16)
                out[pl.ds(pl.multiple_of(offset + at * rows, 8), rows), :] = total
                return carry

            lax.fori_loop(0, take["blocks"], one, 0)


def whole_of(array):
    zeros = (0,) * array.ndim
    return pl.BlockSpec(array.shape, lambda *_: zeros)


def place_in(arrays, array):
    for at, known in enumerate(arrays):
        if known is array:
            return at
    arrays.append(array)
    return len(arrays) - 1


def mix(parts):
    arrays, plan, shapes, pieces = [], [], [], []
    bundles = {}
    for piece, ranges in parts:
        for first, last, digit in ranges:
            rows = last - first
            left, bits = piece.left, 0
            if digit is not None:
                at = piece.left.index(digit)
                left = piece.left[:at] + piece.left[at + 1 :]
                bits = len(left) - at
            blocks = 1 << len(left)
            plan.append(
                dict(
                    kept=place_in(arrays, piece.kept),
                    got=None if piece.got is None else place_in(arrays, piece.got),
                    got_at=piece.offset,
                    whole=piece.rows,
                    first=first,
                    rows=rows,
                    blocks=blocks,
                    bits=bits,
                    digit=digit,
                    to_kept=len(pieces),
                    to_sent=None,
                    sent_at=bundles.get(digit, 0),
                )
            )
            pieces.append(Piece(left, rows, None, None, bundles.get(digit, 0)))
            shapes.append((blocks * rows, LANES))
            if digit is not None:
                bundles[digit] = bundles.get(digit, 0) + blocks * rows
    links = list(bundles)
    for take in plan:
        if take["digit"] is not None:
            take["to_sent"] = len(pieces) + links.index(take["digit"])
    shapes = shapes + [(bundles[digit], LANES) for digit in links]
    outs = [jax.ShapeDtypeStruct(shape, bf16) for shape in shapes]
    results = pl.pallas_call(
        functools.partial(mix_kernel, plan, len(arrays)),
        in_specs=[pl.BlockSpec(memory_space=pltpu.SMEM)] + [whole_of(array) for array in arrays],
        out_specs=[whole_of(out) for out in outs],
        out_shape=outs,
        compiler_params=settings(24),
        cost_estimate=cost(1e6, 4 * sum(shape[0] for shape in shapes) * LANES),
        name="mix",
    )(my_sides(), *arrays)
    arrived = {}
    for digit, sent in zip(links, results[len(pieces) :]):
        axis, apart = mesh_bits()[digit]
        arrived[digit] = swapped(sent, axis, apart)
    for take, piece, kept in zip(plan, pieces, results):
        piece.kept = kept
        if take["digit"] is None:
            piece.offset = 0
        else:
            piece.got = arrived[take["digit"]]
    return pieces


def finish_kernel(plan, loaded, shapes, offsets_ref, *refs):
    def total_of(take, first, rows):
        start = take["got_at"] + first
        mine = refs[take["kept"]][first : first + rows, :].astype(f32)
        return mine + refs[take["got"]][start : start + rows, :].astype(f32)

    for take in plan[:-1]:
        column = take["column"]
        refs[loaded + take["out"]][:, column : column + LANES] = total_of(take, take["first"], take["rows"])
    total = total_of(plan[-1], 0, 8)
    narrow = pltpu.roll(total, lax.rem(LANES - offsets_ref[0], LANES), 1)
    wide = pltpu.roll(total, lax.rem(LANES - offsets_ref[1], LANES), 1)
    outs = refs[loaded + len(shapes) :]
    for at, out in enumerate(outs[:-1]):
        lane = at // 3 * 128
        out[...] = narrow[at % 3 : at % 3 + 1, lane : lane + out.shape[1]]
    outs[-1][...] = wide[:1, 256 : 256 + outs[-1].shape[1]]


def finish(shapes, panels, vectors, widths):
    arrays, plan = [], []
    for piece, first, out, column in panels + [(vectors, 0, None, 0)]:
        plan.append(
            dict(
                kept=place_in(arrays, piece.kept),
                got=place_in(arrays, piece.got),
                got_at=piece.offset,
                first=first,
                rows=None if out is None else shapes[out][0],
                out=out,
                column=column,
            )
        )
    device = lax.axis_index("half") * lax.axis_size("dp") + lax.axis_index("dp")
    offsets = jnp.stack([device * width % 128 for width in widths]).astype(jnp.int32)
    outs = [jax.ShapeDtypeStruct(shape, f32) for shape in shapes]
    outs += [jax.ShapeDtypeStruct((1, width), f32) for width in (widths[0],) * 6 + (widths[1],)]
    return pl.pallas_call(
        functools.partial(finish_kernel, plan, len(arrays), shapes),
        in_specs=[pl.BlockSpec(memory_space=pltpu.SMEM)] + [whole_of(array) for array in arrays],
        out_specs=[whole_of(out) for out in outs],
        out_shape=outs,
        compiler_params=settings(16),
        cost_estimate=cost(1e6, 8e6),
        name="finish",
    )(offsets, *arrays)


def vector_kernel(devices, core_ref, one, two, up, sent, kept):
    even = core_ref[0] == 0
    zero = jnp.zeros((8, 128), f32)

    def block(device):
        narrow = slice(device * one.shape[1] // devices // 128 * 128, None)
        wide = slice(device * up.shape[1] // devices // 128 * 128, None)
        at = slice(narrow.start, narrow.start + 128)
        up_at = slice(wide.start, wide.start + 128)
        top = jnp.concatenate([one[:, at], two[:, at], jnp.broadcast_to(up[:, up_at], (8, 128)), zero], axis=1)
        return jnp.concatenate([top, jnp.zeros_like(top)], axis=0)

    for pair in range(devices // 2):
        first, second = block(2 * pair), block(2 * pair + 1)
        rows = slice(pair * VECTOR_ROWS, (pair + 1) * VECTOR_ROWS)
        sent[rows, :] = jnp.where(even, second, first).astype(bf16)
        kept[rows, :] = jnp.where(even, first, second).astype(bf16)


def vector_piece(core, one, two, up):
    devices = lax.axis_size("half") * lax.axis_size("dp")
    shape = jax.ShapeDtypeStruct((devices // 2 * VECTOR_ROWS, LANES), bf16)
    sent, kept = pl.pallas_call(
        functools.partial(vector_kernel, devices),
        in_specs=[pl.BlockSpec(memory_space=pltpu.SMEM)] + [whole_of(each) for each in (one, two, up)],
        out_specs=[whole_of(shape), whole_of(shape)],
        out_shape=[shape, shape],
        compiler_params=settings(12),
        cost_estimate=cost(1e5, 1e6),
        name="vectors",
    )(core, one, two, up)
    return started(sent, kept)


class Sent:
    def __init__(self, value, axis, apart):
        self.got = swapped(value, axis, apart)


def in_order(values, arrived=(), ready=()):
    gots = []
    for piece in arrived:
        place_in(gots, piece.got)
    kepts = tuple(piece.kept for piece in ready)
    tied = lax.optimization_barrier((tuple(values), tuple(gots), kepts))
    places = [place_in(gots, piece.got) for piece in arrived]
    for piece, place in zip(arrived, places):
        piece.got = tied[1][place]
    for piece, kept in zip(ready, tied[2]):
        piece.kept = kept
    return tied[0]


def split_rows(total, core, rows_each):
    rows, columns = total.shape
    cut = total.reshape(rows // (2 * rows_each), 2, rows_each, columns)
    first, second = cut[:, 0], cut[:, 1]
    even = core == 0
    return jnp.where(even, second, first).astype(bf16), jnp.where(even, first, second).astype(bf16)


def panels_of(blocks, panels, rows_each):
    spec = pl.BlockSpec((blocks, None, rows_each, LANES), lambda i: (0, i, 0, 0))
    return spec, jax.ShapeDtypeStruct((blocks, panels, rows_each, LANES), bf16)


def row_stats(values):
    mean = jnp.mean(values, axis=-1, keepdims=True)
    centred = values - mean
    scale = lax.rsqrt(jnp.mean(centred * centred, axis=-1, keepdims=True) + epsilon)
    return centred * scale, scale


def norm_back(values, gain, grad):
    normal, scale = row_stats(values)
    inner = grad * gain
    along = jnp.mean(inner * normal, axis=-1, keepdims=True)
    return scale * (inner - jnp.mean(inner, axis=-1, keepdims=True) - normal * along), grad * normal


def add_rows(out_ref, *each):
    @pl.when(pl.program_id(0) == 0)
    def _():
        out_ref[...] = jnp.zeros_like(out_ref)

    for row, values in enumerate(each):
        out_ref[row : row + 1, :] += jnp.sum(values, axis=0, keepdims=True)


def enter_kernel(part, mirror, merge, gain, shift, qkv, *rest):
    hidden, normed, projected = rest[-3:]
    value = part[...] + nn(mirror[...], merge[...])
    hidden[...] = value
    low = (row_stats(value)[0] * gain[...] + shift[...]).astype(bf16)
    normed[...] = low
    projected[...] = nn(low, qkv[...]).astype(bf16)


def enter(start, part, mirror, merge_low, gain, shift, qkv, before):
    tokens = part.shape[0]
    offset = start // TILE
    at = lambda columns: pl.BlockSpec((TILE, columns), lambda i: (offset + i, 0))
    operands = (part, mirror, merge_low, gain, shift, qkv)
    return pl.pallas_call(
        enter_kernel,
        grid=(mirror.shape[0] // TILE,),
        in_specs=[at(D), tiled(D), held((D, D)), held((1, D)), held((1, D)), held((D, 3 * D))]
        + [pl.BlockSpec(memory_space=pl.ANY)] * len(before),
        out_specs=[at(D), at(D), at(3 * D)],
        out_shape=[
            pltpu.HBM((tokens, D), f32),
            pltpu.HBM((tokens, D), bf16),
            pltpu.HBM((tokens, 3 * D), bf16),
        ],
        input_output_aliases={len(operands) + i: i for i in range(len(before))},
        compiler_params=settings(22),
        cost_estimate=cost(8 * mirror.shape[0] * D * D, 26 * MIB),
        name="enter",
    )(*operands, *before)


def leave_kernel(hidden, mixed, out_weight, gain, shift, residual, normed):
    value = hidden[...] + nn(mixed[...], out_weight[...])
    residual[...] = value
    normed[...] = (row_stats(value)[0] * gain[...] + shift[...]).astype(bf16)


def leave(hidden, mixed, out_weight, gain, shift):
    tokens = hidden.shape[0]
    return pl.pallas_call(
        leave_kernel,
        grid=(tokens // TILE,),
        in_specs=[tiled(D), tiled(D), held((D, D)), held((1, D)), held((1, D))],
        out_specs=[tiled(D), tiled(D)],
        out_shape=[pltpu.HBM((tokens, D), f32), pltpu.HBM((tokens, D), bf16)],
        compiler_params=settings(16),
        cost_estimate=cost(2 * tokens * D * D, 14 * MIB),
        name="leave",
    )(hidden, mixed, out_weight, gain, shift)


def windows(lengths):
    ends = jnp.cumsum(lengths, axis=1)
    starts = ends - lengths
    low = (jnp.arange(BLOCKS, dtype=jnp.int32) * BLOCK)[None, :, None]
    holds_low = (low >= starts[:, None, :]) & (low < ends[:, None, :])
    high = low + (BLOCK - 1)
    holds_high = (high >= starts[:, None, :]) & (high < ends[:, None, :])
    window_low = jnp.sum(jnp.where(holds_low, starts[:, None, :], 0), axis=2) // BLOCK
    window_high = (jnp.sum(jnp.where(holds_high, ends[:, None, :], 0), axis=2) + BLOCK - 1) // BLOCK
    return window_low.reshape(-1), (window_high - window_low).reshape(-1)


def row_segments(lengths):
    ends = jnp.cumsum(lengths, axis=1)
    position = jnp.arange(ROW_LEN, dtype=jnp.int32)
    return jnp.sum((position[None, :, None] >= ends[:, None, :]).astype(jnp.int32), axis=2)


def head_slopes():
    return jnp.array([2.0 ** (-8.0 * (head + 1.0) / H) for head in range(H)], f32)


def fill_distance(far_ref, column, line):
    for b in range(BLOCKS):
        rows = slice(b * BLOCK, (b + 1) * BLOCK)
        i = lax.broadcasted_iota(jnp.int32, (BLOCK, ROW_LEN), 0) + b * BLOCK
        j = lax.broadcasted_iota(jnp.int32, (BLOCK, ROW_LEN), 1)
        distance = jnp.abs(i - j).astype(f32)
        far_ref[rows, :] = jnp.where(column[rows, :] == line[...], distance, FAR)


def masked_pair(value, lows):
    zero = jnp.zeros_like(value)
    return jnp.concatenate([jnp.where(lows, value, zero), jnp.where(lows, zero, value)], axis=0)


def over_blocks(low_ref, count_ref, row, variant):
    def block(b, carry):
        rows = pl.ds(pl.multiple_of(b * BLOCK, BLOCK), BLOCK)
        start = pl.multiple_of(low_ref[row * BLOCKS + b] * BLOCK, BLOCK)
        count = count_ref[row * BLOCKS + b]
        for n in range(1, BLOCKS + 1):
            pl.when(count == n)(functools.partial(variant, rows, pl.ds(start, n * BLOCK)))
        return carry

    lax.fori_loop(0, BLOCKS, block, 0)


def attend_kernel(
    low_ref, count_ref, slope_ref, column, line, q_ref, k_ref, v_ref, o_ref, lse_ref, far_ref, value_ref
):
    row = pl.program_id(0)
    group = pl.program_id(1)

    @pl.when(group == 0)
    def _():
        fill_distance(far_ref, column, line)
        lse_ref[...] = jnp.zeros_like(lse_ref)

    lane = lax.broadcasted_iota(jnp.int32, (1, 128), 1)
    lows = lane < HD
    for pair in range(HEADS // 2):
        value_ref[pair, :, :128] = v_ref[:, pair * 128 : pair * 128 + 128]
        value_ref[pair, :, 128:] = jnp.ones((ROW_LEN, 128), bf16)

    def variant(rows, cols):
        far = far_ref[rows, cols]
        logs = lse_ref[rows, :]
        for pair in range(HEADS // 2):
            at = slice(pair * 128, pair * 128 + 128)
            head = group * HEADS + pair * 2
            query = masked_pair(q_ref[rows, at] * bf16(HD**-0.5), lows)
            score = nt(query, k_ref[cols, at])
            score = score - jnp.concatenate([slope_ref[head] * far, slope_ref[head + 1] * far], axis=0)
            top = jnp.max(score, axis=1, keepdims=True)
            soft = jnp.exp(score - top).astype(bf16)
            both = nn(soft, value_ref[pair, cols, :])
            total = both[:, 128:]
            log_total = top + jnp.log(total)
            logs = jnp.where(lane == head, log_total[:BLOCK], logs)
            logs = jnp.where(lane == head + 1, log_total[BLOCK:], logs)
            mixed = jnp.where(lows, both[:BLOCK, :128], both[BLOCK:, :128])
            o_ref[rows, at] = (mixed / jnp.where(lows, total[:BLOCK], total[BLOCK:])).astype(bf16)
        lse_ref[rows, :] = logs

    over_blocks(low_ref, count_ref, row, variant)


def head_group(part):
    return pl.BlockSpec((ROW_LEN, HEADS * HD), lambda r, g, *_: (r, part * GROUPS + g))


def attention_operands(lengths):
    rows = lengths.shape[0]
    segments = row_segments(lengths)
    return windows(lengths) + (
        head_slopes(),
        segments.reshape(rows * ROW_LEN, 1),
        segments.reshape(rows, 1, ROW_LEN),
    )


def segment_specs():
    return [
        pl.BlockSpec((ROW_LEN, 1), lambda r, *_: (r, 0)),
        pl.BlockSpec((None, 1, ROW_LEN), lambda r, *_: (r, 0, 0)),
    ]


def attend(projected, operands):
    tokens = projected.shape[0]
    rows = tokens // ROW_LEN
    return launch(
        attend_kernel,
        operands + (projected, projected, projected),
        scalars=3,
        out_shape=[jax.ShapeDtypeStruct((tokens, D), bf16), jax.ShapeDtypeStruct((tokens, 128), f32)],
        grid=(rows, GROUPS),
        in_specs=segment_specs() + [head_group(0), head_group(1), head_group(2)],
        out_specs=[head_group(0), pl.BlockSpec((ROW_LEN, 128), lambda r, g, *_: (r, 0))],
        scratch_shapes=[
            pltpu.VMEM((ROW_LEN, ROW_LEN), f32),
            pltpu.VMEM((HEADS // 2, ROW_LEN, 256), bf16),
        ],
        compiler_params=settings(48),
        cost_estimate=cost(rows * 20e9, 30 * MIB),
        name="attend",
    )


def attend_back_kernel(
    group,
    low_ref,
    count_ref,
    slope_ref,
    column,
    line,
    q_ref,
    k_ref,
    v_ref,
    grad_ref,
    lse_ref,
    delta_ref,
    out_ref,
    far_ref,
    turned_ref,
    key_ref,
):
    row = pl.program_id(0)
    fill_distance(far_ref, column, line)
    lows = lax.broadcasted_iota(jnp.int32, (1, 128), 1) < HD
    tops = lax.broadcasted_iota(jnp.int32, (128, 1), 0) < HD
    turned_ref[...] = jnp.zeros_like(turned_ref)
    for pair in range(HEADS // 2):
        key_ref[pair] = k_ref[:, pair * 128 : pair * 128 + 128].T

    def variant(rows, cols):
        far = far_ref[rows, cols]
        for pair in range(HEADS // 2):
            at = slice(pair * 128, pair * 128 + 128)
            head = group * HEADS + pair * 2
            query = q_ref[cols, at] * bf16(HD**-0.5)
            grad = grad_ref[cols, at]
            score = nt(masked_pair(k_ref[rows, at], lows), query)
            soft_grad = nt(masked_pair(v_ref[rows, at], lows), grad)
            softs, score_grads = [], []
            for side in range(2):
                part = slice(side * BLOCK, side * BLOCK + BLOCK)
                own = pl.ds(pair * 2 + side, 1)
                soft = jnp.exp(score[part] - slope_ref[head + side] * far - lse_ref[own, cols])
                score_grads.append((soft * (soft_grad[part] - delta_ref[own, cols])).astype(bf16))
                softs.append(soft.astype(bf16))
            score_grad = jnp.concatenate(score_grads, axis=0)
            value_grad = nn(jnp.concatenate(softs, axis=0), grad)
            key_grad = nn(score_grad, query)
            out_ref[2, rows, at] = jnp.where(lows, value_grad[:BLOCK], value_grad[BLOCK:]).astype(bf16)
            out_ref[1, rows, at] = jnp.where(lows, key_grad[:BLOCK], key_grad[BLOCK:]).astype(bf16)
            key = key_ref[pair, :, rows]
            zero = jnp.zeros_like(key)
            keys = jnp.concatenate([jnp.where(tops, key, zero), jnp.where(tops, zero, key)], axis=1)
            turned_ref[at, cols] += nn(keys, score_grad)

    over_blocks(low_ref, count_ref, row, variant)
    out_ref[0] = (turned_ref[...].T * HD**-0.5).astype(bf16)


def attend_back(group, projected, grad, lse_rows, delta_rows, operands, pins):
    tokens = projected.shape[0]
    rows = tokens // ROW_LEN
    of_group = lambda part: pl.BlockSpec((ROW_LEN, HEADS * HD), lambda r, *_: (r, part * GROUPS + group))
    thin = pl.BlockSpec((None, HEADS, ROW_LEN), lambda r, *_: (r, group, 0))
    return launch(
        functools.partial(attend_back_kernel, group),
        operands + (projected, projected, projected, grad, lse_rows, delta_rows),
        pins,
        scalars=3,
        out_shape=jax.ShapeDtypeStruct((3, tokens, HEADS * HD), bf16),
        grid=(rows,),
        in_specs=segment_specs() + [of_group(0), of_group(1), of_group(2), of_group(0), thin, thin],
        out_specs=pl.BlockSpec((3, ROW_LEN, HEADS * HD), lambda r, *_: (0, r, 0)),
        scratch_shapes=[
            pltpu.VMEM((ROW_LEN, ROW_LEN), f32),
            pltpu.VMEM((HEADS * HD, ROW_LEN), f32),
            pltpu.VMEM((HEADS // 2, 128, ROW_LEN), bf16),
        ],
        compiler_params=settings(26),
        cost_estimate=cost(rows * 18e9, 16 * MIB),
        name="attend_back",
    )


PULL = 0.44
ERFC = (
    0.1241083994,
    0.1244657618,
    0.1084788423,
    0.1084610390,
    -0.0110834557,
    0.1493682951,
    -0.1395405297,
    0.0357417408,
)


def gelu_pair(value):
    size = jnp.abs(value)
    t = 1.0 / (1.0 + (PULL * 0.5**0.5) * size)
    poly = jnp.full_like(t, ERFC[-1])
    for term in reversed(ERFC[:-1]):
        poly = poly * t + term
    bell = jnp.exp(value * value * -0.5)
    tail = bell * t * poly
    whole = jnp.where(value < 0, tail, 1.0 - tail)
    return value * whole, whole + value * (bell * (0.5 / jnp.pi) ** 0.5)


def feed_kernel(
    rows_up,
    rows_down,
    core_ref,
    normed,
    cotangent,
    up_weight,
    up_bias,
    back,
    activated,
    normed_grad,
    bias_grad,
    up_sent,
    up_kept,
    down_sent,
    down_kept,
):
    core = core_ref[0]

    @pl.when(pl.program_id(0) == 0)
    def _():
        normed_grad[...] = jnp.zeros_like(normed_grad)

    value = nn(normed[...], up_weight[...]) + up_bias[...]
    active, slope = gelu_pair(value)
    active = active.astype(bf16)
    activated[...] = active
    grad = (back[...].astype(f32) * slope).astype(bf16)
    bias_grad[...] = jnp.sum(grad.astype(f32), axis=0, keepdims=True)
    normed_grad[...] += nt(grad, up_weight[...])
    for value, out in zip(split_rows(tn(active, cotangent[...]), core, rows_down), (down_sent, down_kept)):
        for panel in range(D // LANES):
            out[:, panel] = value[:, :, panel * LANES : panel * LANES + LANES]
    up_sent[...], up_kept[...] = split_rows(tn(normed[...], grad), core, rows_up)


def feed(core, normed, cotangent, up_weight, up_bias, back, width=LANES):
    tokens = normed.shape[0]
    hidden_units = up_weight.shape[1]
    devices = lax.axis_size("half") * lax.axis_size("dp")
    across = lambda rows: pl.BlockSpec((rows, width), lambda i: (0, i))
    shape = jax.ShapeDtypeStruct
    up_spec, up_shape = panels_of(devices // 2, hidden_units // LANES, D // devices)
    rows_down = hidden_units // devices
    down_spec = pl.BlockSpec((width // (2 * rows_down), D // LANES, rows_down, LANES), lambda i: (i, 0, 0, 0))
    down_shape = shape((devices // 2, D // LANES, rows_down, LANES), bf16)
    return launch(
        functools.partial(feed_kernel, D // devices, hidden_units // devices),
        (core, normed, cotangent, up_weight, up_bias, back),
        grid=(hidden_units // width,),
        in_specs=[
            pl.BlockSpec(memory_space=pltpu.SMEM),
            held((tokens, D)),
            held((tokens, D)),
            across(D),
            across(1),
            across(tokens),
        ],
        out_specs=[
            across(tokens),
            pl.BlockSpec((tokens, D), lambda i: (0, 0)),
            across(1),
            up_spec,
            up_spec,
            down_spec,
            down_spec,
        ],
        out_shape=[
            shape((tokens, hidden_units), bf16),
            shape((tokens, D), f32),
            shape((1, hidden_units), f32),
            up_shape,
            up_shape,
            down_shape,
            down_shape,
        ],
        compiler_params=settings(48),
        cost_estimate=cost(8 * tokens * D * hidden_units, 60 * MIB),
        name="feed",
    )


def output_kernel(activated, down_weight, residual, bias, output):
    output[...] = (residual[...] + bias[...] + nn(activated[...], down_weight[...])).astype(bf16)


def layer_output(activated, down_weight, residual, bias, pins):
    tokens, hidden_units = activated.shape
    across = lambda rows: pl.BlockSpec((rows, TILE), lambda i: (0, i))
    return launch(
        output_kernel,
        (activated, down_weight, residual, bias),
        pins,
        grid=(D // TILE,),
        in_specs=[held((tokens, hidden_units)), across(hidden_units), across(tokens), across(1)],
        out_specs=across(tokens),
        out_shape=jax.ShapeDtypeStruct((tokens, D), bf16),
        compiler_params=settings(48),
        cost_estimate=cost(2 * tokens * D * hidden_units, 24 * MIB),
        name="layer_output",
    )


def second_back_kernel(
    normed_grad,
    residual,
    cotangent,
    gain,
    out_weight,
    mixed,
    lse,
    residual_grad,
    attention_grad,
    mixed_grad,
    delta_rows,
    lse_rows,
    sums,
):
    incoming = normed_grad[...]
    outer = cotangent[...].astype(f32)
    through, gain_terms = norm_back(residual[...], gain[...], incoming)
    value = outer + through
    residual_grad[...] = value
    low = value.astype(bf16)
    attention_grad[...] = low
    mixed_low = nt(low, out_weight[...]).astype(bf16)
    mixed_grad[...] = mixed_low
    product = mixed_low.astype(f32) * mixed[...].astype(f32)
    high = product.astype(bf16)
    rest = (product - high.astype(f32)).astype(bf16)
    of_head = lax.broadcasted_iota(jnp.int32, (H, D), 1) // HD
    member = (of_head == lax.broadcasted_iota(jnp.int32, (H, D), 0)).astype(bf16)
    delta_rows[...] = nt(member, high) + nt(member, rest)
    lse_rows[...] = lse[...].T[:H]
    add_rows(sums, gain_terms, incoming, outer)


def second_back(normed_grad, residual, cotangent, gain, out_weight, mixed, lse):
    tokens = residual.shape[0]
    per_row = ROW_LEN // TILE
    shape = jax.ShapeDtypeStruct
    thin = pl.BlockSpec((None, H, TILE), lambda i: (i // per_row, 0, i % per_row))
    return pl.pallas_call(
        second_back_kernel,
        grid=(tokens // TILE,),
        in_specs=[tiled(D), tiled(D), tiled(D), held((1, D)), held((D, D)), tiled(D), tiled(128)],
        out_specs=[tiled(D), tiled(D), tiled(D), thin, thin, summed_over(D)],
        out_shape=[
            shape((tokens, D), f32),
            shape((tokens, D), bf16),
            shape((tokens, D), bf16),
            shape((tokens // ROW_LEN, H, ROW_LEN), f32),
            shape((tokens // ROW_LEN, H, ROW_LEN), f32),
            shape((8, D), f32),
        ],
        compiler_params=settings(48),
        cost_estimate=cost(3 * tokens * D * D, 22 * MIB),
        name="second_back",
    )(normed_grad, residual, cotangent, gain, out_weight, mixed, lse)


def first_back_kernel(
    first, second, hidden, residual_grad, gain, qkv, hidden_grad, sums
):
    incoming = jnp.zeros(hidden.shape, f32)
    wide = HEADS * HD
    for part in range(3):
        for at, grad in enumerate((first, second)):
            start = part * D + at * wide
            incoming += nt(grad[part], qkv[:, start : start + wide])
    through, gain_terms = norm_back(hidden[...], gain[...], incoming)
    low = (residual_grad[...] + through).astype(bf16)
    hidden_grad[...] = low
    add_rows(sums, gain_terms, incoming, low.astype(f32))


def first_back(projected_grads, hidden, residual_grad, gain, qkv, pins):
    tokens = hidden.shape[0]
    shape = jax.ShapeDtypeStruct
    group = pl.BlockSpec((3, TILE, HEADS * HD), lambda i: (0, i, 0))
    return launch(
        first_back_kernel,
        projected_grads + (hidden, residual_grad, gain, qkv),
        pins,
        grid=(tokens // TILE,),
        in_specs=[group, group, tiled(D), tiled(D), held((1, D)), held((D, 3 * D))],
        out_specs=[tiled(D), summed_over(D)],
        out_shape=[shape((tokens, D), bf16), shape((8, D), f32)],
        compiler_params=settings(20),
        cost_estimate=cost(6 * tokens * D * D, 22 * MIB),
        name="first_back",
    )


def joined_kernel(grad, merge, out):
    out[...] = nt(grad[...], merge[...]).astype(bf16)


def joined_grad(hidden_grad, merge_half, pins, name):
    tokens = hidden_grad.shape[0]
    return launch(
        joined_kernel,
        (hidden_grad, merge_half),
        pins,
        grid=(tokens // TILE,),
        in_specs=[tiled(D), held((D, D))],
        out_specs=tiled(D),
        out_shape=jax.ShapeDtypeStruct((tokens, D), bf16),
        compiler_params=settings(12),
        cost_estimate=cost(2 * tokens * D * D, 6 * MIB),
        name=name,
    )


def weight_kernel(rows_each, core_ref, left, right, sent, kept):
    sent[...], kept[...] = split_rows(tn(left[...], right[...]), core_ref[0], rows_each)


def merge_kernel(rows_each, core_ref, frames, *refs):
    mirrors, (right, sent, kept) = refs[:-3], refs[-3:]
    half = sent.shape[0] // 2
    sent[:half], kept[:half] = split_rows(tn(frames[...], right[...]), core_ref[0], rows_each)
    total = jnp.zeros((D, right.shape[1]), f32)
    start = 0
    for mirror in mirrors:
        end = start + mirror.shape[0]
        total += tn(mirror[...], right[start:end, :])
        start = end
    sent[half:], kept[half:] = split_rows(total, core_ref[0], rows_each)


def merge_grad(core, frames, mirrors, right, width=LANES):
    tokens = frames.shape[0]
    devices = lax.axis_size("half") * lax.axis_size("dp")
    out, out_shape = panels_of(devices // 2, D // width, 2 * D // devices)
    return launch(
        functools.partial(merge_kernel, 2 * D // devices),
        (core, frames, *mirrors, right),
        grid=(D // width,),
        in_specs=[pl.BlockSpec(memory_space=pltpu.SMEM), held((tokens, D))]
        + [held(mirror.shape) for mirror in mirrors]
        + [pl.BlockSpec((tokens, width), lambda i: (0, i))],
        out_specs=[out, out],
        out_shape=[out_shape, out_shape],
        compiler_params=settings(18),
        cost_estimate=cost(4 * tokens * D * D, 16 * MIB),
        name="merge_grad",
    )


def weight_grad(core, left, right, name):
    tokens = left.shape[0]
    devices = lax.axis_size("half") * lax.axis_size("dp")
    spec = pl.BlockSpec((tokens, LANES), lambda i: (0, i))
    panels = right.shape[-1] // LANES
    if right.ndim == 3:
        spec = pl.BlockSpec((None, tokens, LANES), lambda i: (i, 0, 0))
        panels = right.shape[0]
    out, out_shape = panels_of(devices // 2, panels, D // devices)
    return launch(
        functools.partial(weight_kernel, D // devices),
        (core, left, right),
        grid=(panels,),
        in_specs=[pl.BlockSpec(memory_space=pltpu.SMEM), held((tokens, D)), spec],
        out_specs=[out, out],
        out_shape=[out_shape, out_shape],
        compiler_params=settings(18),
        cost_estimate=cost(2 * tokens * D * LANES * panels, 16 * MIB),
        name=name,
    )


def on_device(
    frames,
    skip_rows,
    lengths,
    merge_weight,
    merge_bias,
    norm1_gain,
    norm1_bias,
    qkv_weight,
    out_weight,
    norm2_gain,
    norm2_bias,
    up_weight,
    up_bias,
    down_weight,
    down_bias,
    cotangent,
):
    tokens = frames.shape[0]
    line = lambda vector: vector.reshape(1, -1)
    core = (lax.axis_index("dp") & 1).astype(jnp.int32).reshape(1)
    mirrors = []
    for start, end in zip(CUTS[:-1], CUTS[1:]):
        piece = skip_rows[start:end]
        if mirrors:
            piece, mirrors[-1] = lax.optimization_barrier((piece, mirrors[-1]))
        mirrors.append(swapped(piece, "half", 0))
    operands = attention_operands(lengths)
    back = nt(cotangent, down_weight).astype(bf16)
    part = nn(frames, merge_weight[:D]) + merge_bias
    entered = ()
    for start, mirror in zip(CUTS, mirrors):
        entered = enter(
            start, part, mirror, merge_weight[D:], line(norm1_gain), line(norm1_bias), qkv_weight, entered
        )
    hidden, normed, projected = entered
    mixed, lse = attend(projected, operands)
    residual, normed_two = leave(hidden, mixed, out_weight, line(norm2_gain), line(norm2_bias))
    activated, normed_two_grad, up_bias_grad, up_sent, up_kept, down_sent, down_kept = feed(
        core, normed_two, cotangent, up_weight, line(up_bias), back
    )
    _, x, y, (l, *deep) = digits()
    down = started(down_sent, down_kept)
    up = started(up_sent, up_kept)
    residual_grad, attention_grad, mixed_grad, delta_rows, lse_rows, sums_two = second_back(
        normed_two_grad, residual, cotangent, line(norm2_gain), out_weight, mixed, lse
    )
    out = started(*weight_grad(core, mixed, attention_grad, "out_grad"))
    (mixed_grad,) = in_order((mixed_grad,), (down,), (out,))
    panel = D // (lax.axis_size("half") * lax.axis_size("dp"))
    h = deep[0]
    cut, end = down.rows // 2, down.rows
    one, two = mix([(down, ((0, cut, x), (cut, end, y)))])
    (mixed_grad,) = in_order((mixed_grad,), (up,), (one, two))
    cut, end = up.rows // 2, up.rows
    three, rest = mix([(up, ((0, cut, l), (cut, end, None)))])
    (mixed_grad,) = in_order((mixed_grad,), (), (three, rest))
    first = attend_back(0, projected, mixed_grad, lse_rows, delta_rows, operands, ())
    (first,) = in_order((first,), (one, two, three, out))
    query = started(*weight_grad(core, normed, first, "query_grad"))
    (one.kept,) = in_order((one.kept,), (), (query,))
    cut, end = rest.rows // 2, rest.rows
    one, two, three, four, five, out = mix(
        [
            (one, cuts(one, y)),
            (two, cuts(two, l)),
            (three, cuts(three, x)),
            (rest, ((0, cut, y), (cut, end, l))),
            (out, cuts(out, x)),
        ]
    )
    (mixed_grad,) = in_order((mixed_grad,), (), (one, two, three, four, five, out))
    second = attend_back(1, projected, mixed_grad, lse_rows, delta_rows, operands, ())
    (second,) = in_order((second,), (one, two, three, four, five, out, query))
    later = started(*weight_grad(core, normed, second, "query_grad"))
    (one.kept,) = in_order((one.kept,), (), (later,))
    one, two, three, four, five, out, query_one, query_two = mix(
        [
            (one, cuts(one, l)),
            (two, cuts(two, x)),
            (three, cuts(three, y)),
            (four, cuts(four, x)),
            (five, cuts(five, y)),
            (out, cuts(out, y)),
            (query, ((0, panel, x), (panel, 3 * panel, l))),
        ]
    )
    (second,) = in_order((second,), (), (one, two, three, four, five, out, query_one, query_two))
    hidden_grad, sums_one = first_back(
        (first, second), hidden, residual_grad, line(norm1_gain), qkv_weight, ()
    )
    skip_part = joined_grad(hidden_grad, merge_weight[D:], (), "skip_grad")
    (hidden_grad, skip_part, sums_one) = in_order(
        (hidden_grad, skip_part, sums_one), (one, two, three, four, five, out, query_one, query_two, later)
    )
    skip = Sent(skip_part, "half", 0)
    one, two, three, four, five, out, query_one, query_two, later_one, later_two = mix(
        [
            (one, cuts(one, h)),
            (two, cuts(two, h)),
            (three, cuts(three, h)),
            (four, cuts(four, l)),
            (five, cuts(five, h)),
            (out, cuts(out, l)),
            (query_one, cuts(query_one, y)),
            (query_two, cuts(query_two, y)),
            (later, ((0, 2 * panel, y), (2 * panel, 3 * panel, l))),
        ]
    )
    vectors = vector_piece(core, sums_one, sums_two, up_bias_grad)
    (hidden_grad,) = in_order((hidden_grad,), (), (four, out, query_one, query_two, later_one, later_two, vectors))
    merge = started(*merge_grad(core, frames, mirrors, hidden_grad))
    (hidden_grad,) = in_order((hidden_grad,), (), (merge,))
    frames_grad = joined_grad(hidden_grad, merge_weight[:D], (), "frames_grad")
    (frames_grad, residual) = in_order(
        (frames_grad, residual), (four, out, query_one, query_two, later_one, later_two, vectors, merge)
    )
    cut, end = merge.rows // 2, merge.rows
    merge_one, merge_two, vectors = mix([(merge, ((0, cut, y), (cut, end, l))), (vectors, cuts(vectors, y))])
    (residual,) = in_order((residual,), (), (merge_one, merge_two, vectors))
    output = layer_output(activated, down_weight, residual, line(down_bias), ())
    (output,) = in_order((output,), (merge_one, merge_two, vectors, one, two, three, five))
    moving = mix(
        [
            (four, cuts(four, h)),
            (five, cuts(five, x)),
            (out, cuts(out, h)),
            (query_one, cuts(query_one, l)),
            (query_two, cuts(query_two, x)),
            (later_one, cuts(later_one, x)),
            (later_two, cuts(later_two, y)),
            (merge_one, cuts(merge_one, l)),
            (merge_two, cuts(merge_two, y)),
            (vectors, cuts(vectors, l)),
        ]
    )
    four, five, out, query_one, query_two, later_one, later_two, merge_one, merge_two, vectors = moving
    (vectors.kept,) = in_order((vectors.kept,), moving + [skip])
    moving = mix(
        [
            (query_one, cuts(query_one, h)),
            (query_two, cuts(query_two, h)),
            (later_one, cuts(later_one, l)),
            (later_two, cuts(later_two, x)),
            (merge_one, cuts(merge_one, x)),
            (merge_two, cuts(merge_two, x)),
            (vectors, cuts(vectors, x)),
        ]
    )
    query_one, query_two, later_one, later_two, merge_one, merge_two, vectors = moving
    skip_grad = moved(skip.got)
    (vectors.kept, skip_grad) = in_order((vectors.kept, skip_grad), moving)
    later_one, later_two, merge_one, merge_two, vectors = mix(
        [(each, cuts(each, h)) for each in (later_one, later_two, merge_one, merge_two, vectors)]
    )
    pieces = [one, two, three, four, five, out, query_one, query_two, later_one, later_two]
    pieces += [merge_one, merge_two, vectors]
    while any(piece.left for piece in pieces):
        open_pieces = [piece for piece in pieces if piece.left]
        closed = mix([(piece, cuts(piece, piece.left[0])) for piece in open_pieces])
        pieces = [closed.pop(0) if piece.left else piece for piece in pieces]
    one, two, three, four, five, out, query_one, query_two, later_one, later_two = pieces[:10]
    merge_one, merge_two, vectors = pieces[10:]
    devices = lax.axis_size("half") * lax.axis_size("dp")
    hidden_units = up_weight.shape[1]
    wide = HEADS * HD
    per = three.rows // panel
    plan = [(one, 0, 0, 0), (two, 0, 0, LANES)]
    plan += [(three, at * panel, 1, at * LANES) for at in range(per)]
    plan += [(four, at * panel, 1, (per + at) * LANES) for at in range(per // 2)]
    plan += [(five, at * panel, 1, (per + per // 2 + at) * LANES) for at in range(per // 2)]
    plan += [(out, 0, 2, 0), (out, panel, 2, LANES)]
    plan += [(query_one, 0, 3, 0), (query_two, 0, 3, D), (query_two, panel, 3, 2 * D)]
    plan += [(later_one, 0, 3, wide), (later_one, panel, 3, D + wide), (later_two, 0, 3, 2 * D + wide)]
    plan += [(merge_one, 0, 4, 0), (merge_two, 0, 4, LANES)]
    down_weight_grad, up_weight_grad, out_weight_grad, qkv_weight_grad, merge_weight_grad, *small = finish(
        [
            (hidden_units // devices, D),
            (D // devices, hidden_units),
            (D // devices, D),
            (D // devices, 3 * D),
            (2 * D // devices, D),
        ],
        plan,
        vectors,
        (D // devices, hidden_units // devices),
    )
    gain_one, shift_one, merge_bias_grad, gain_two, shift_two, down_bias_grad, up_bias_grad = [
        each.reshape(-1) for each in small
    ]
    return (
        output,
        frames_grad,
        skip_grad,
        merge_weight_grad,
        merge_bias_grad,
        gain_one,
        shift_one,
        qkv_weight_grad,
        out_weight_grad,
        gain_two,
        shift_two,
        up_weight_grad,
        up_bias_grad,
        down_weight_grad,
        down_bias_grad,
    )


def moved_kernel(source, target):
    target[...] = source[...]


def moved(value):
    rows = pl.BlockSpec((TILE, D), lambda i: (i, 0))
    return pl.pallas_call(
        moved_kernel,
        grid=(value.shape[0] // TILE,),
        in_specs=[rows],
        out_specs=rows,
        out_shape=jax.ShapeDtypeStruct(value.shape, value.dtype),
        compiler_params=settings(12),
        name="moved",
    )(value)


def cuts(piece, digit):
    return ((0, piece.rows, digit),)


def solution(mesh):
    rows = P(("half", "dp"), None)
    parts = P(("half", "dp"))
    in_specs = (rows, rows, rows) + (P(),) * 12 + (rows,)
    out_specs = (rows, rows, rows, rows, parts, parts, parts, rows, rows, parts, parts, rows, parts, rows, parts)
    return jax.shard_map(
        on_device, mesh=mesh, in_specs=in_specs, out_specs=out_specs, check_vma=False
    )
```

```python
import functools

import jax
import jax.numpy as jnp
from jax import lax
from jax.experimental import pallas as pl
from jax.experimental.pallas import tpu as pltpu
from jax.sharding import PartitionSpec as P

D = 1024
H = 16
HD = 64
ROW_LEN = 1024
BLOCK = 128
BLOCKS = ROW_LEN // BLOCK
TILE = 256
CUTS = (0, 768, 1024)
LANES = 512
VECTOR_ROWS = 16
HEADS = 8
GROUPS = H // HEADS
FAR = 1e30
epsilon = 1e-05
f32 = jnp.float32
bf16 = jnp.bfloat16
MIB = 1024 * 1024


def nn(left, right):
    return jnp.dot(left, right, preferred_element_type=f32)


def nt(left, right):
    return lax.dot_general(left, right, (((1,), (1,)), ((), ())), preferred_element_type=f32)


def tn(left, right):
    return lax.dot_general(left, right, (((0,), (0,)), ((), ())), preferred_element_type=f32)


def settings(megabytes):
    return pltpu.CompilerParams(vmem_limit_bytes=megabytes * MIB)


def cost(flops, moved):
    return pl.CostEstimate(flops=int(flops), bytes_accessed=int(moved), transcendentals=0)


def held(shape):
    zeros = (0,) * len(shape)
    return pl.BlockSpec(shape, lambda *_: zeros, pipeline_mode=pl.Buffered(1))


def tiled(columns):
    return pl.BlockSpec((TILE, columns), lambda i: (i, 0))


def summed_over(columns):
    return pl.BlockSpec((8, columns), lambda i: (0, 0))


def launch(kernel, operands, pins=(), in_specs=(), scalars=0, **rest):
    count, extra = len(operands), len(pins)

    def body(*refs):
        kernel(*refs[:count], *refs[count + extra :])

    in_specs = list(in_specs) + [pl.BlockSpec(memory_space=pl.ANY)] * extra
    if scalars:
        rest["grid_spec"] = pltpu.PrefetchScalarGridSpec(
            num_scalar_prefetch=scalars,
            grid=rest.pop("grid"),
            in_specs=in_specs,
            out_specs=rest.pop("out_specs"),
            scratch_shapes=rest.pop("scratch_shapes"),
        )
    else:
        rest["in_specs"] = in_specs
    return pl.pallas_call(body, **rest)(*operands, *pins)


def swapped(value, axis, apart):
    mask = 2**apart
    pairs = [(source, source ^ mask) for source in range(lax.axis_size(axis))]
    return lax.ppermute(value, axis, pairs)


def mesh_bits():
    dp_bits = lax.axis_size("dp").bit_length() - 1
    half_bits = lax.axis_size("half").bit_length() - 1
    return [("half", bit) for bit in reversed(range(half_bits))] + [
        ("dp", bit) for bit in reversed(range(dp_bits))
    ]


def digits():
    count = len(mesh_bits())
    return count - 1, 0, count - 2, list(range(count - 3, 0, -1))


def my_sides():
    return jnp.stack([(lax.axis_index(axis) >> apart) & 1 for axis, apart in mesh_bits()]).astype(jnp.int32)


class Piece:
    def __init__(self, left, rows, kept, got=None, offset=0):
        self.left, self.rows, self.kept, self.got, self.offset = tuple(left), rows, kept, got, offset


def started(sent, kept):
    count = len(mesh_bits()) - 1
    flat = lambda value: value.reshape(-1, LANES)
    kept = flat(kept)
    return Piece(range(count), kept.shape[0] >> count, kept, swapped(flat(sent), "dp", 0))


def mix_kernel(plan, loaded, sides_ref, *refs):
    for take in plan:
        low, rows = take["bits"], take["rows"]
        for to, offset, other in ((take["to_sent"], take["sent_at"], True), (take["to_kept"], 0, False)):
            if to is None:
                continue
            out = refs[loaded + to]
            side = None
            if take["digit"] is not None:
                side = sides_ref[take["digit"]]
                side = 1 - side if other else side

            def one(at, carry, side=side, out=out, offset=offset, take=take, low=low, rows=rows):
                block = at if side is None else ((((at >> low) * 2) + side) << low) + (at & ((1 << low) - 1))
                start = block * take["whole"] + take["first"]
                total = refs[take["kept"]][pl.ds(pl.multiple_of(start, 8), rows), :]
                if take["got"] is not None:
                    theirs = refs[take["got"]][pl.ds(pl.multiple_of(take["got_at"] + start, 8), rows), :]
                    total = (total.astype(f32) + theirs.astype(f32)).astype(bf16)
                out[pl.ds(pl.multiple_of(offset + at * rows, 8), rows), :] = total
                return carry

            lax.fori_loop(0, take["blocks"], one, 0)


def whole_of(array):
    zeros = (0,) * array.ndim
    return pl.BlockSpec(array.shape, lambda *_: zeros)


def place_in(arrays, array):
    for at, known in enumerate(arrays):
        if known is array:
            return at
    arrays.append(array)
    return len(arrays) - 1


def mix(parts):
    arrays, plan, shapes, pieces = [], [], [], []
    bundles = {}
    for piece, ranges in parts:
        for first, last, digit in ranges:
            rows = last - first
            left, bits = piece.left, 0
            if digit is not None:
                at = piece.left.index(digit)
                left = piece.left[:at] + piece.left[at + 1 :]
                bits = len(left) - at
            blocks = 1 << len(left)
            plan.append(
                dict(
                    kept=place_in(arrays, piece.kept),
                    got=None if piece.got is None else place_in(arrays, piece.got),
                    got_at=piece.offset,
                    whole=piece.rows,
                    first=first,
                    rows=rows,
                    blocks=blocks,
                    bits=bits,
                    digit=digit,
                    to_kept=len(pieces),
                    to_sent=None,
                    sent_at=bundles.get(digit, 0),
                )
            )
            pieces.append(Piece(left, rows, None, None, bundles.get(digit, 0)))
            shapes.append((blocks * rows, LANES))
            if digit is not None:
                bundles[digit] = bundles.get(digit, 0) + blocks * rows
    links = list(bundles)
    for take in plan:
        if take["digit"] is not None:
            take["to_sent"] = len(pieces) + links.index(take["digit"])
    shapes = shapes + [(bundles[digit], LANES) for digit in links]
    outs = [jax.ShapeDtypeStruct(shape, bf16) for shape in shapes]
    results = pl.pallas_call(
        functools.partial(mix_kernel, plan, len(arrays)),
        in_specs=[pl.BlockSpec(memory_space=pltpu.SMEM)] + [whole_of(array) for array in arrays],
        out_specs=[whole_of(out) for out in outs],
        out_shape=outs,
        compiler_params=settings(24),
        cost_estimate=cost(1e6, 4 * sum(shape[0] for shape in shapes) * LANES),
        name="mix",
    )(my_sides(), *arrays)
    arrived = {}
    for digit, sent in zip(links, results[len(pieces) :]):
        axis, apart = mesh_bits()[digit]
        arrived[digit] = swapped(sent, axis, apart)
    for take, piece, kept in zip(plan, pieces, results):
        piece.kept = kept
        if take["digit"] is None:
            piece.offset = 0
        else:
            piece.got = arrived[take["digit"]]
    return pieces


def finish_kernel(plan, loaded, shapes, offsets_ref, *refs):
    def total_of(take, first, rows):
        start = take["got_at"] + first
        mine = refs[take["kept"]][first : first + rows, :].astype(f32)
        return mine + refs[take["got"]][start : start + rows, :].astype(f32)

    for take in plan[:-1]:
        column = take["column"]
        refs[loaded + take["out"]][:, column : column + LANES] = total_of(take, take["first"], take["rows"])
    total = total_of(plan[-1], 0, 8)
    narrow = pltpu.roll(total, lax.rem(LANES - offsets_ref[0], LANES), 1)
    wide = pltpu.roll(total, lax.rem(LANES - offsets_ref[1], LANES), 1)
    outs = refs[loaded + len(shapes) :]
    for at, out in enumerate(outs[:-1]):
        lane = at // 3 * 128
        out[...] = narrow[at % 3 : at % 3 + 1, lane : lane + out.shape[1]]
    outs[-1][...] = wide[:1, 256 : 256 + outs[-1].shape[1]]


def finish(shapes, panels, vectors, widths):
    arrays, plan = [], []
    for piece, first, out, column in panels + [(vectors, 0, None, 0)]:
        plan.append(
            dict(
                kept=place_in(arrays, piece.kept),
                got=place_in(arrays, piece.got),
                got_at=piece.offset,
                first=first,
                rows=None if out is None else shapes[out][0],
                out=out,
                column=column,
            )
        )
    device = lax.axis_index("half") * lax.axis_size("dp") + lax.axis_index("dp")
    offsets = jnp.stack([device * width % 128 for width in widths]).astype(jnp.int32)
    outs = [jax.ShapeDtypeStruct(shape, f32) for shape in shapes]
    outs += [jax.ShapeDtypeStruct((1, width), f32) for width in (widths[0],) * 6 + (widths[1],)]
    return pl.pallas_call(
        functools.partial(finish_kernel, plan, len(arrays), shapes),
        in_specs=[pl.BlockSpec(memory_space=pltpu.SMEM)] + [whole_of(array) for array in arrays],
        out_specs=[whole_of(out) for out in outs],
        out_shape=outs,
        compiler_params=settings(16),
        cost_estimate=cost(1e6, 8e6),
        name="finish",
    )(offsets, *arrays)


def vector_kernel(devices, core_ref, one, two, up, sent, kept):
    even = core_ref[0] == 0
    zero = jnp.zeros((8, 128), f32)

    def block(device):
        narrow = slice(device * one.shape[1] // devices // 128 * 128, None)
        wide = slice(device * up.shape[1] // devices // 128 * 128, None)
        at = slice(narrow.start, narrow.start + 128)
        up_at = slice(wide.start, wide.start + 128)
        top = jnp.concatenate([one[:, at], two[:, at], jnp.broadcast_to(up[:, up_at], (8, 128)), zero], axis=1)
        return jnp.concatenate([top, jnp.zeros_like(top)], axis=0)

    for pair in range(devices // 2):
        first, second = block(2 * pair), block(2 * pair + 1)
        rows = slice(pair * VECTOR_ROWS, (pair + 1) * VECTOR_ROWS)
        sent[rows, :] = jnp.where(even, second, first).astype(bf16)
        kept[rows, :] = jnp.where(even, first, second).astype(bf16)


def vector_piece(core, one, two, up):
    devices = lax.axis_size("half") * lax.axis_size("dp")
    shape = jax.ShapeDtypeStruct((devices // 2 * VECTOR_ROWS, LANES), bf16)
    sent, kept = pl.pallas_call(
        functools.partial(vector_kernel, devices),
        in_specs=[pl.BlockSpec(memory_space=pltpu.SMEM)] + [whole_of(each) for each in (one, two, up)],
        out_specs=[whole_of(shape), whole_of(shape)],
        out_shape=[shape, shape],
        compiler_params=settings(12),
        cost_estimate=cost(1e5, 1e6),
        name="vectors",
    )(core, one, two, up)
    return started(sent, kept)


class Sent:
    def __init__(self, value, axis, apart):
        self.got = swapped(value, axis, apart)


def in_order(values, arrived=(), ready=()):
    gots = []
    for piece in arrived:
        place_in(gots, piece.got)
    kepts = tuple(piece.kept for piece in ready)
    tied = lax.optimization_barrier((tuple(values), tuple(gots), kepts))
    places = [place_in(gots, piece.got) for piece in arrived]
    for piece, place in zip(arrived, places):
        piece.got = tied[1][place]
    for piece, kept in zip(ready, tied[2]):
        piece.kept = kept
    return tied[0]


def split_rows(total, core, rows_each):
    rows, columns = total.shape
    cut = total.reshape(rows // (2 * rows_each), 2, rows_each, columns)
    first, second = cut[:, 0], cut[:, 1]
    even = core == 0
    return jnp.where(even, second, first).astype(bf16), jnp.where(even, first, second).astype(bf16)


def panels_of(blocks, panels, rows_each):
    spec = pl.BlockSpec((blocks, None, rows_each, LANES), lambda i: (0, i, 0, 0))
    return spec, jax.ShapeDtypeStruct((blocks, panels, rows_each, LANES), bf16)


def row_stats(values):
    mean = jnp.mean(values, axis=-1, keepdims=True)
    centred = values - mean
    scale = lax.rsqrt(jnp.mean(centred * centred, axis=-1, keepdims=True) + epsilon)
    return centred * scale, scale


def norm_back(values, gain, grad):
    normal, scale = row_stats(values)
    inner = grad * gain
    along = jnp.mean(inner * normal, axis=-1, keepdims=True)
    return scale * (inner - jnp.mean(inner, axis=-1, keepdims=True) - normal * along), grad * normal


def add_rows(out_ref, *each):
    @pl.when(pl.program_id(0) == 0)
    def _():
        out_ref[...] = jnp.zeros_like(out_ref)

    for row, values in enumerate(each):
        out_ref[row : row + 1, :] += jnp.sum(values, axis=0, keepdims=True)


def enter_kernel(part, mirror, merge, gain, shift, qkv, *rest):
    hidden, normed, projected = rest[-3:]
    value = part[...] + nn(mirror[...], merge[...])
    hidden[...] = value
    low = (row_stats(value)[0] * gain[...] + shift[...]).astype(bf16)
    normed[...] = low
    projected[...] = nn(low, qkv[...]).astype(bf16)


def enter(start, part, mirror, merge_low, gain, shift, qkv, before):
    tokens = part.shape[0]
    offset = start // TILE
    at = lambda columns: pl.BlockSpec((TILE, columns), lambda i: (offset + i, 0))
    operands = (part, mirror, merge_low, gain, shift, qkv)
    return pl.pallas_call(
        enter_kernel,
        grid=(mirror.shape[0] // TILE,),
        in_specs=[at(D), tiled(D), held((D, D)), held((1, D)), held((1, D)), held((D, 3 * D))]
        + [pl.BlockSpec(memory_space=pl.ANY)] * len(before),
        out_specs=[at(D), at(D), at(3 * D)],
        out_shape=[
            pltpu.HBM((tokens, D), f32),
            pltpu.HBM((tokens, D), bf16),
            pltpu.HBM((tokens, 3 * D), bf16),
        ],
        input_output_aliases={len(operands) + i: i for i in range(len(before))},
        compiler_params=settings(22),
        cost_estimate=cost(8 * mirror.shape[0] * D * D, 26 * MIB),
        name="enter",
    )(*operands, *before)


def leave_kernel(hidden, mixed, out_weight, gain, shift, residual, normed):
    value = hidden[...] + nn(mixed[...], out_weight[...])
    residual[...] = value
    normed[...] = (row_stats(value)[0] * gain[...] + shift[...]).astype(bf16)


def leave(hidden, mixed, out_weight, gain, shift):
    tokens = hidden.shape[0]
    return pl.pallas_call(
        leave_kernel,
        grid=(tokens // TILE,),
        in_specs=[tiled(D), tiled(D), held((D, D)), held((1, D)), held((1, D))],
        out_specs=[tiled(D), tiled(D)],
        out_shape=[pltpu.HBM((tokens, D), f32), pltpu.HBM((tokens, D), bf16)],
        compiler_params=settings(16),
        cost_estimate=cost(2 * tokens * D * D, 14 * MIB),
        name="leave",
    )(hidden, mixed, out_weight, gain, shift)


def windows(lengths):
    ends = jnp.cumsum(lengths, axis=1)
    starts = ends - lengths
    low = (jnp.arange(BLOCKS, dtype=jnp.int32) * BLOCK)[None, :, None]
    holds_low = (low >= starts[:, None, :]) & (low < ends[:, None, :])
    high = low + (BLOCK - 1)
    holds_high = (high >= starts[:, None, :]) & (high < ends[:, None, :])
    window_low = jnp.sum(jnp.where(holds_low, starts[:, None, :], 0), axis=2) // BLOCK
    window_high = (jnp.sum(jnp.where(holds_high, ends[:, None, :], 0), axis=2) + BLOCK - 1) // BLOCK
    return window_low.reshape(-1), (window_high - window_low).reshape(-1)


def row_segments(lengths):
    ends = jnp.cumsum(lengths, axis=1)
    position = jnp.arange(ROW_LEN, dtype=jnp.int32)
    return jnp.sum((position[None, :, None] >= ends[:, None, :]).astype(jnp.int32), axis=2)


def head_slopes():
    return jnp.array([2.0 ** (-8.0 * (head + 1.0) / H) for head in range(H)], f32)


def fill_distance(far_ref, column, line):
    for b in range(BLOCKS):
        rows = slice(b * BLOCK, (b + 1) * BLOCK)
        i = lax.broadcasted_iota(jnp.int32, (BLOCK, ROW_LEN), 0) + b * BLOCK
        j = lax.broadcasted_iota(jnp.int32, (BLOCK, ROW_LEN), 1)
        distance = jnp.abs(i - j).astype(f32)
        far_ref[rows, :] = jnp.where(column[rows, :] == line[...], distance, FAR)


def masked_pair(value, lows):
    zero = jnp.zeros_like(value)
    return jnp.concatenate([jnp.where(lows, value, zero), jnp.where(lows, zero, value)], axis=0)


def over_blocks(low_ref, count_ref, row, variant):
    def block(b, carry):
        rows = pl.ds(pl.multiple_of(b * BLOCK, BLOCK), BLOCK)
        start = pl.multiple_of(low_ref[row * BLOCKS + b] * BLOCK, BLOCK)
        count = count_ref[row * BLOCKS + b]
        for n in range(1, BLOCKS + 1):
            pl.when(count == n)(functools.partial(variant, rows, pl.ds(start, n * BLOCK)))
        return carry

    lax.fori_loop(0, BLOCKS, block, 0)


def attend_kernel(
    low_ref, count_ref, slope_ref, column, line, q_ref, k_ref, v_ref, o_ref, lse_ref, far_ref, value_ref
):
    row = pl.program_id(0)
    group = pl.program_id(1)

    @pl.when(group == 0)
    def _():
        fill_distance(far_ref, column, line)
        lse_ref[...] = jnp.zeros_like(lse_ref)

    lane = lax.broadcasted_iota(jnp.int32, (1, 128), 1)
    lows = lane < HD
    for pair in range(HEADS // 2):
        value_ref[pair, :, :128] = v_ref[:, pair * 128 : pair * 128 + 128]
        value_ref[pair, :, 128:] = jnp.ones((ROW_LEN, 128), bf16)

    def variant(rows, cols):
        far = far_ref[rows, cols]
        logs = lse_ref[rows, :]
        for pair in range(HEADS // 2):
            at = slice(pair * 128, pair * 128 + 128)
            head = group * HEADS + pair * 2
            query = masked_pair(q_ref[rows, at] * bf16(HD**-0.5), lows)
            score = nt(query, k_ref[cols, at])
            score = score - jnp.concatenate([slope_ref[head] * far, slope_ref[head + 1] * far], axis=0)
            top = jnp.max(score, axis=1, keepdims=True)
            soft = jnp.exp(score - top).astype(bf16)
            both = nn(soft, value_ref[pair, cols, :])
            total = both[:, 128:]
            log_total = top + jnp.log(total)
            logs = jnp.where(lane == head, log_total[:BLOCK], logs)
            logs = jnp.where(lane == head + 1, log_total[BLOCK:], logs)
            mixed = jnp.where(lows, both[:BLOCK, :128], both[BLOCK:, :128])
            o_ref[rows, at] = (mixed / jnp.where(lows, total[:BLOCK], total[BLOCK:])).astype(bf16)
        lse_ref[rows, :] = logs

    over_blocks(low_ref, count_ref, row, variant)


def head_group(part):
    return pl.BlockSpec((ROW_LEN, HEADS * HD), lambda r, g, *_: (r, part * GROUPS + g))


def attention_operands(lengths):
    rows = lengths.shape[0]
    segments = row_segments(lengths)
    return windows(lengths) + (
        head_slopes(),
        segments.reshape(rows * ROW_LEN, 1),
        segments.reshape(rows, 1, ROW_LEN),
    )


def segment_specs():
    return [
        pl.BlockSpec((ROW_LEN, 1), lambda r, *_: (r, 0)),
        pl.BlockSpec((None, 1, ROW_LEN), lambda r, *_: (r, 0, 0)),
    ]


def attend(projected, operands):
    tokens = projected.shape[0]
    rows = tokens // ROW_LEN
    return launch(
        attend_kernel,
        operands + (projected, projected, projected),
        scalars=3,
        out_shape=[jax.ShapeDtypeStruct((tokens, D), bf16), jax.ShapeDtypeStruct((tokens, 128), f32)],
        grid=(rows, GROUPS),
        in_specs=segment_specs() + [head_group(0), head_group(1), head_group(2)],
        out_specs=[head_group(0), pl.BlockSpec((ROW_LEN, 128), lambda r, g, *_: (r, 0))],
        scratch_shapes=[
            pltpu.VMEM((ROW_LEN, ROW_LEN), f32),
            pltpu.VMEM((HEADS // 2, ROW_LEN, 256), bf16),
        ],
        compiler_params=settings(48),
        cost_estimate=cost(rows * 20e9, 30 * MIB),
        name="attend",
    )


def attend_back_kernel(
    group,
    low_ref,
    count_ref,
    slope_ref,
    column,
    line,
    q_ref,
    k_ref,
    v_ref,
    grad_ref,
    lse_ref,
    delta_ref,
    out_ref,
    far_ref,
    turned_ref,
    key_ref,
):
    row = pl.program_id(0)
    fill_distance(far_ref, column, line)
    lows = lax.broadcasted_iota(jnp.int32, (1, 128), 1) < HD
    tops = lax.broadcasted_iota(jnp.int32, (128, 1), 0) < HD
    turned_ref[...] = jnp.zeros_like(turned_ref)
    for pair in range(HEADS // 2):
        key_ref[pair] = k_ref[:, pair * 128 : pair * 128 + 128].T

    def variant(rows, cols):
        far = far_ref[rows, cols]
        for pair in range(HEADS // 2):
            at = slice(pair * 128, pair * 128 + 128)
            head = group * HEADS + pair * 2
            query = q_ref[cols, at] * bf16(HD**-0.5)
            grad = grad_ref[cols, at]
            score = nt(masked_pair(k_ref[rows, at], lows), query)
            soft_grad = nt(masked_pair(v_ref[rows, at], lows), grad)
            softs, score_grads = [], []
            for side in range(2):
                part = slice(side * BLOCK, side * BLOCK + BLOCK)
                own = pl.ds(pair * 2 + side, 1)
                soft = jnp.exp(score[part] - slope_ref[head + side] * far - lse_ref[own, cols])
                score_grads.append((soft * (soft_grad[part] - delta_ref[own, cols])).astype(bf16))
                softs.append(soft.astype(bf16))
            score_grad = jnp.concatenate(score_grads, axis=0)
            value_grad = nn(jnp.concatenate(softs, axis=0), grad)
            key_grad = nn(score_grad, query)
            out_ref[2, rows, at] = jnp.where(lows, value_grad[:BLOCK], value_grad[BLOCK:]).astype(bf16)
            out_ref[1, rows, at] = jnp.where(lows, key_grad[:BLOCK], key_grad[BLOCK:]).astype(bf16)
            key = key_ref[pair, :, rows]
            zero = jnp.zeros_like(key)
            keys = jnp.concatenate([jnp.where(tops, key, zero), jnp.where(tops, zero, key)], axis=1)
            turned_ref[at, cols] += nn(keys, score_grad)

    over_blocks(low_ref, count_ref, row, variant)
    out_ref[0] = (turned_ref[...].T * HD**-0.5).astype(bf16)


def attend_back(group, projected, grad, lse_rows, delta_rows, operands, pins):
    tokens = projected.shape[0]
    rows = tokens // ROW_LEN
    of_group = lambda part: pl.BlockSpec((ROW_LEN, HEADS * HD), lambda r, *_: (r, part * GROUPS + group))
    thin = pl.BlockSpec((None, HEADS, ROW_LEN), lambda r, *_: (r, group, 0))
    return launch(
        functools.partial(attend_back_kernel, group),
        operands + (projected, projected, projected, grad, lse_rows, delta_rows),
        pins,
        scalars=3,
        out_shape=jax.ShapeDtypeStruct((3, tokens, HEADS * HD), bf16),
        grid=(rows,),
        in_specs=segment_specs() + [of_group(0), of_group(1), of_group(2), of_group(0), thin, thin],
        out_specs=pl.BlockSpec((3, ROW_LEN, HEADS * HD), lambda r, *_: (0, r, 0)),
        scratch_shapes=[
            pltpu.VMEM((ROW_LEN, ROW_LEN), f32),
            pltpu.VMEM((HEADS * HD, ROW_LEN), f32),
            pltpu.VMEM((HEADS // 2, 128, ROW_LEN), bf16),
        ],
        compiler_params=settings(26),
        cost_estimate=cost(rows * 18e9, 16 * MIB),
        name="attend_back",
    )


PULL = 0.44
ERFC = (
    0.1241083994,
    0.1244657618,
    0.1084788423,
    0.1084610390,
    -0.0110834557,
    0.1493682951,
    -0.1395405297,
    0.0357417408,
)


def gelu_pair(value):
    size = jnp.abs(value)
    t = 1.0 / (1.0 + (PULL * 0.5**0.5) * size)
    poly = jnp.full_like(t, ERFC[-1])
    for term in reversed(ERFC[:-1]):
        poly = poly * t + term
    bell = jnp.exp(value * value * -0.5)
    tail = bell * t * poly
    whole = jnp.where(value < 0, tail, 1.0 - tail)
    return value * whole, whole + value * (bell * (0.5 / jnp.pi) ** 0.5)


def feed_kernel(
    rows_up,
    rows_down,
    core_ref,
    normed,
    cotangent,
    up_weight,
    up_bias,
    back,
    activated,
    normed_grad,
    bias_grad,
    up_sent,
    up_kept,
    down_sent,
    down_kept,
):
    core = core_ref[0]

    @pl.when(pl.program_id(0) == 0)
    def _():
        normed_grad[...] = jnp.zeros_like(normed_grad)

    value = nn(normed[...], up_weight[...]) + up_bias[...]
    active, slope = gelu_pair(value)
    active = active.astype(bf16)
    activated[...] = active
    grad = (back[...].astype(f32) * slope).astype(bf16)
    bias_grad[...] = jnp.sum(grad.astype(f32), axis=0, keepdims=True)
    normed_grad[...] += nt(grad, up_weight[...])
    for value, out in zip(split_rows(tn(active, cotangent[...]), core, rows_down), (down_sent, down_kept)):
        for panel in range(D // LANES):
            out[:, panel] = value[:, :, panel * LANES : panel * LANES + LANES]
    up_sent[...], up_kept[...] = split_rows(tn(normed[...], grad), core, rows_up)


def feed(core, normed, cotangent, up_weight, up_bias, back, width=LANES):
    tokens = normed.shape[0]
    hidden_units = up_weight.shape[1]
    devices = lax.axis_size("half") * lax.axis_size("dp")
    across = lambda rows: pl.BlockSpec((rows, width), lambda i: (0, i))
    shape = jax.ShapeDtypeStruct
    up_spec, up_shape = panels_of(devices // 2, hidden_units // LANES, D // devices)
    rows_down = hidden_units // devices
    down_spec = pl.BlockSpec((width // (2 * rows_down), D // LANES, rows_down, LANES), lambda i: (i, 0, 0, 0))
    down_shape = shape((devices // 2, D // LANES, rows_down, LANES), bf16)
    return launch(
        functools.partial(feed_kernel, D // devices, hidden_units // devices),
        (core, normed, cotangent, up_weight, up_bias, back),
        grid=(hidden_units // width,),
        in_specs=[
            pl.BlockSpec(memory_space=pltpu.SMEM),
            held((tokens, D)),
            held((tokens, D)),
            across(D),
            across(1),
            across(tokens),
        ],
        out_specs=[
            across(tokens),
            pl.BlockSpec((tokens, D), lambda i: (0, 0)),
            across(1),
            up_spec,
            up_spec,
            down_spec,
            down_spec,
        ],
        out_shape=[
            shape((tokens, hidden_units), bf16),
            shape((tokens, D), f32),
            shape((1, hidden_units), f32),
            up_shape,
            up_shape,
            down_shape,
            down_shape,
        ],
        compiler_params=settings(48),
        cost_estimate=cost(8 * tokens * D * hidden_units, 60 * MIB),
        name="feed",
    )


def output_kernel(activated, down_weight, residual, bias, output):
    output[...] = (residual[...] + bias[...] + nn(activated[...], down_weight[...])).astype(bf16)


def layer_output(activated, down_weight, residual, bias, pins):
    tokens, hidden_units = activated.shape
    across = lambda rows: pl.BlockSpec((rows, TILE), lambda i: (0, i))
    return launch(
        output_kernel,
        (activated, down_weight, residual, bias),
        pins,
        grid=(D // TILE,),
        in_specs=[held((tokens, hidden_units)), across(hidden_units), across(tokens), across(1)],
        out_specs=across(tokens),
        out_shape=jax.ShapeDtypeStruct((tokens, D), bf16),
        compiler_params=settings(48),
        cost_estimate=cost(2 * tokens * D * hidden_units, 24 * MIB),
        name="layer_output",
    )


def second_back_kernel(
    normed_grad,
    residual,
    cotangent,
    gain,
    out_weight,
    mixed,
    lse,
    attention_grad,
    mixed_grad,
    delta_rows,
    lse_rows,
    sums,
):
    incoming = normed_grad[...]
    outer = cotangent[...].astype(f32)
    through, gain_terms = norm_back(residual[...], gain[...], incoming)
    low = (outer + through).astype(bf16)
    attention_grad[...] = low
    mixed_low = nt(low, out_weight[...]).astype(bf16)
    mixed_grad[...] = mixed_low
    product = mixed_low.astype(f32) * mixed[...].astype(f32)
    high = product.astype(bf16)
    rest = (product - high.astype(f32)).astype(bf16)
    of_head = lax.broadcasted_iota(jnp.int32, (H, D), 1) // HD
    member = (of_head == lax.broadcasted_iota(jnp.int32, (H, D), 0)).astype(bf16)
    delta_rows[...] = nt(member, high) + nt(member, rest)
    lse_rows[...] = lse[...].T[:H]
    add_rows(sums, gain_terms, incoming, outer)


def second_back(normed_grad, residual, cotangent, gain, out_weight, mixed, lse):
    tokens = residual.shape[0]
    per_row = ROW_LEN // TILE
    shape = jax.ShapeDtypeStruct
    thin = pl.BlockSpec((None, H, TILE), lambda i: (i // per_row, 0, i % per_row))
    return pl.pallas_call(
        second_back_kernel,
        grid=(tokens // TILE,),
        in_specs=[tiled(D), tiled(D), tiled(D), held((1, D)), held((D, D)), tiled(D), tiled(128)],
        out_specs=[tiled(D), tiled(D), thin, thin, summed_over(D)],
        out_shape=[
            shape((tokens, D), bf16),
            shape((tokens, D), bf16),
            shape((tokens // ROW_LEN, H, ROW_LEN), f32),
            shape((tokens // ROW_LEN, H, ROW_LEN), f32),
            shape((8, D), f32),
        ],
        compiler_params=settings(48),
        cost_estimate=cost(3 * tokens * D * D, 22 * MIB),
        name="second_back",
    )(normed_grad, residual, cotangent, gain, out_weight, mixed, lse)


def first_back_kernel(
    first, second, hidden, outer_grad, gain, qkv, hidden_grad, sums
):
    incoming = jnp.zeros(hidden.shape, f32)
    wide = HEADS * HD
    for part in range(3):
        for at, grad in enumerate((first, second)):
            start = part * D + at * wide
            incoming += nt(grad[part], qkv[:, start : start + wide])
    through, gain_terms = norm_back(hidden[...], gain[...], incoming)
    low = (outer_grad[...].astype(f32) + through).astype(bf16)
    hidden_grad[...] = low
    add_rows(sums, gain_terms, incoming, low.astype(f32))


def first_back(projected_grads, hidden, outer_grad, gain, qkv, pins):
    tokens = hidden.shape[0]
    shape = jax.ShapeDtypeStruct
    group = pl.BlockSpec((3, TILE, HEADS * HD), lambda i: (0, i, 0))
    return launch(
        first_back_kernel,
        projected_grads + (hidden, outer_grad, gain, qkv),
        pins,
        grid=(tokens // TILE,),
        in_specs=[group, group, tiled(D), tiled(D), held((1, D)), held((D, 3 * D))],
        out_specs=[tiled(D), summed_over(D)],
        out_shape=[shape((tokens, D), bf16), shape((8, D), f32)],
        compiler_params=settings(20),
        cost_estimate=cost(6 * tokens * D * D, 22 * MIB),
        name="first_back",
    )


def joined_kernel(grad, merge, out):
    out[...] = nt(grad[...], merge[...]).astype(bf16)


def joined_grad(hidden_grad, merge_half, pins, name):
    tokens = hidden_grad.shape[0]
    return launch(
        joined_kernel,
        (hidden_grad, merge_half),
        pins,
        grid=(tokens // TILE,),
        in_specs=[tiled(D), held((D, D))],
        out_specs=tiled(D),
        out_shape=jax.ShapeDtypeStruct((tokens, D), bf16),
        compiler_params=settings(12),
        cost_estimate=cost(2 * tokens * D * D, 6 * MIB),
        name=name,
    )


def weight_kernel(rows_each, core_ref, left, right, sent, kept):
    sent[...], kept[...] = split_rows(tn(left[...], right[...]), core_ref[0], rows_each)


def merge_kernel(rows_each, core_ref, frames, *refs):
    mirrors, (right, sent, kept) = refs[:-3], refs[-3:]
    half = sent.shape[0] // 2
    sent[:half], kept[:half] = split_rows(tn(frames[...], right[...]), core_ref[0], rows_each)
    total = jnp.zeros((D, right.shape[1]), f32)
    start = 0
    for mirror in mirrors:
        end = start + mirror.shape[0]
        total += tn(mirror[...], right[start:end, :])
        start = end
    sent[half:], kept[half:] = split_rows(total, core_ref[0], rows_each)


def merge_grad(core, frames, mirrors, right, width=LANES):
    tokens = frames.shape[0]
    devices = lax.axis_size("half") * lax.axis_size("dp")
    out, out_shape = panels_of(devices // 2, D // width, 2 * D // devices)
    return launch(
        functools.partial(merge_kernel, 2 * D // devices),
        (core, frames, *mirrors, right),
        grid=(D // width,),
        in_specs=[pl.BlockSpec(memory_space=pltpu.SMEM), held((tokens, D))]
        + [held(mirror.shape) for mirror in mirrors]
        + [pl.BlockSpec((tokens, width), lambda i: (0, i))],
        out_specs=[out, out],
        out_shape=[out_shape, out_shape],
        compiler_params=settings(18),
        cost_estimate=cost(4 * tokens * D * D, 16 * MIB),
        name="merge_grad",
    )


def weight_grad(core, left, right, name):
    tokens = left.shape[0]
    devices = lax.axis_size("half") * lax.axis_size("dp")
    spec = pl.BlockSpec((tokens, LANES), lambda i: (0, i))
    panels = right.shape[-1] // LANES
    if right.ndim == 3:
        spec = pl.BlockSpec((None, tokens, LANES), lambda i: (i, 0, 0))
        panels = right.shape[0]
    out, out_shape = panels_of(devices // 2, panels, D // devices)
    return launch(
        functools.partial(weight_kernel, D // devices),
        (core, left, right),
        grid=(panels,),
        in_specs=[pl.BlockSpec(memory_space=pltpu.SMEM), held((tokens, D)), spec],
        out_specs=[out, out],
        out_shape=[out_shape, out_shape],
        compiler_params=settings(18),
        cost_estimate=cost(2 * tokens * D * LANES * panels, 16 * MIB),
        name=name,
    )


def on_device(
    frames,
    skip_rows,
    lengths,
    merge_weight,
    merge_bias,
    norm1_gain,
    norm1_bias,
    qkv_weight,
    out_weight,
    norm2_gain,
    norm2_bias,
    up_weight,
    up_bias,
    down_weight,
    down_bias,
    cotangent,
):
    tokens = frames.shape[0]
    line = lambda vector: vector.reshape(1, -1)
    core = (lax.axis_index("dp") & 1).astype(jnp.int32).reshape(1)
    mirrors = []
    for start, end in zip(CUTS[:-1], CUTS[1:]):
        piece = skip_rows[start:end]
        if mirrors:
            piece, mirrors[-1] = lax.optimization_barrier((piece, mirrors[-1]))
        mirrors.append(swapped(piece, "half", 0))
    operands = attention_operands(lengths)
    back = nt(cotangent, down_weight).astype(bf16)
    part = nn(frames, merge_weight[:D]) + merge_bias
    entered = ()
    for start, mirror in zip(CUTS, mirrors):
        entered = enter(
            start, part, mirror, merge_weight[D:], line(norm1_gain), line(norm1_bias), qkv_weight, entered
        )
    hidden, normed, projected = entered
    mixed, lse = attend(projected, operands)
    residual, normed_two = leave(hidden, mixed, out_weight, line(norm2_gain), line(norm2_bias))
    activated, normed_two_grad, up_bias_grad, up_sent, up_kept, down_sent, down_kept = feed(
        core, normed_two, cotangent, up_weight, line(up_bias), back
    )
    _, x, y, (l, *deep) = digits()
    down = started(down_sent, down_kept)
    up = started(up_sent, up_kept)
    attention_grad, mixed_grad, delta_rows, lse_rows, sums_two = second_back(
        normed_two_grad, residual, cotangent, line(norm2_gain), out_weight, mixed, lse
    )
    out = started(*weight_grad(core, mixed, attention_grad, "out_grad"))
    (mixed_grad,) = in_order((mixed_grad,), (down,), (out,))
    panel = D // (lax.axis_size("half") * lax.axis_size("dp"))
    h = deep[0]
    cut, end = down.rows // 2, down.rows
    one, two = mix([(down, ((0, cut, x), (cut, end, y)))])
    (mixed_grad,) = in_order((mixed_grad,), (up,), (one, two))
    cut, end = up.rows // 2, up.rows
    three, rest = mix([(up, ((0, cut, l), (cut, end, None)))])
    (mixed_grad,) = in_order((mixed_grad,), (), (three, rest))
    first = attend_back(0, projected, mixed_grad, lse_rows, delta_rows, operands, ())
    (first,) = in_order((first,), (one, two, three, out))
    query = started(*weight_grad(core, normed, first, "query_grad"))
    (one.kept,) = in_order((one.kept,), (), (query,))
    cut, end = rest.rows // 2, rest.rows
    one, two, three, four, five, out = mix(
        [
            (one, cuts(one, y)),
            (two, cuts(two, l)),
            (three, cuts(three, x)),
            (rest, ((0, cut, y), (cut, end, l))),
            (out, cuts(out, x)),
        ]
    )
    (mixed_grad,) = in_order((mixed_grad,), (), (one, two, three, four, five, out))
    second = attend_back(1, projected, mixed_grad, lse_rows, delta_rows, operands, ())
    (second,) = in_order((second,), (one, two, three, four, five, out, query))
    later = started(*weight_grad(core, normed, second, "query_grad"))
    (one.kept,) = in_order((one.kept,), (), (later,))
    one, two, three, four, five, out, query_one, query_two = mix(
        [
            (one, cuts(one, l)),
            (two, cuts(two, x)),
            (three, cuts(three, y)),
            (four, cuts(four, x)),
            (five, cuts(five, y)),
            (out, cuts(out, y)),
            (query, ((0, panel, x), (panel, 3 * panel, l))),
        ]
    )
    (second,) = in_order((second,), (), (one, two, three, four, five, out, query_one, query_two))
    hidden_grad, sums_one = first_back(
        (first, second), hidden, attention_grad, line(norm1_gain), qkv_weight, ()
    )
    skip_part = joined_grad(hidden_grad, merge_weight[D:], (), "skip_grad")
    (hidden_grad, skip_part, sums_one) = in_order(
        (hidden_grad, skip_part, sums_one), (one, two, three, four, five, out, query_one, query_two, later)
    )
    skip = Sent(skip_part, "half", 0)
    one, two, three, four, five, out, query_one, query_two, later_one, later_two = mix(
        [
            (one, cuts(one, h)),
            (two, cuts(two, h)),
            (three, cuts(three, h)),
            (four, cuts(four, l)),
            (five, cuts(five, h)),
            (out, cuts(out, l)),
            (query_one, cuts(query_one, y)),
            (query_two, cuts(query_two, y)),
            (later, ((0, 2 * panel, y), (2 * panel, 3 * panel, l))),
        ]
    )
    vectors = vector_piece(core, sums_one, sums_two, up_bias_grad)
    (hidden_grad,) = in_order((hidden_grad,), (), (four, out, query_one, query_two, later_one, later_two, vectors))
    merge = started(*merge_grad(core, frames, mirrors, hidden_grad))
    (hidden_grad,) = in_order((hidden_grad,), (), (merge,))
    frames_grad = joined_grad(hidden_grad, merge_weight[:D], (), "frames_grad")
    (frames_grad, residual) = in_order(
        (frames_grad, residual), (four, out, query_one, query_two, later_one, later_two, vectors, merge)
    )
    cut, end = merge.rows // 2, merge.rows
    merge_one, merge_two, vectors = mix([(merge, ((0, cut, y), (cut, end, l))), (vectors, cuts(vectors, y))])
    (residual,) = in_order((residual,), (), (merge_one, merge_two, vectors))
    output = layer_output(activated, down_weight, residual, line(down_bias), ())
    (output,) = in_order((output,), (merge_one, merge_two, vectors, one, two, three, five))
    moving = mix(
        [
            (four, cuts(four, h)),
            (five, cuts(five, x)),
            (out, cuts(out, h)),
            (query_one, cuts(query_one, l)),
            (query_two, cuts(query_two, x)),
            (later_one, cuts(later_one, x)),
            (later_two, cuts(later_two, y)),
            (merge_one, cuts(merge_one, l)),
            (merge_two, cuts(merge_two, y)),
            (vectors, cuts(vectors, l)),
        ]
    )
    four, five, out, query_one, query_two, later_one, later_two, merge_one, merge_two, vectors = moving
    (vectors.kept,) = in_order((vectors.kept,), moving + [skip])
    moving = mix(
        [
            (query_one, cuts(query_one, h)),
            (query_two, cuts(query_two, h)),
            (later_one, cuts(later_one, l)),
            (later_two, cuts(later_two, x)),
            (merge_one, cuts(merge_one, x)),
            (merge_two, cuts(merge_two, h)),
            (vectors, cuts(vectors, x)),
        ]
    )
    query_one, query_two, later_one, later_two, merge_one, merge_two, vectors = moving
    skip_grad = moved(skip.got)
    (vectors.kept, skip_grad) = in_order((vectors.kept, skip_grad), moving)
    later_one, later_two, merge_one, merge_two, vectors = mix(
        [
            (later_one, cuts(later_one, h)),
            (later_two, cuts(later_two, h)),
            (merge_one, cuts(merge_one, h)),
            (merge_two, cuts(merge_two, x)),
            (vectors, cuts(vectors, h)),
        ]
    )
    pieces = [one, two, three, four, five, out, query_one, query_two, later_one, later_two]
    pieces += [merge_one, merge_two, vectors]
    while any(piece.left for piece in pieces):
        open_pieces = [piece for piece in pieces if piece.left]
        closed = mix([(piece, cuts(piece, piece.left[0])) for piece in open_pieces])
        pieces = [closed.pop(0) if piece.left else piece for piece in pieces]
    one, two, three, four, five, out, query_one, query_two, later_one, later_two = pieces[:10]
    merge_one, merge_two, vectors = pieces[10:]
    devices = lax.axis_size("half") * lax.axis_size("dp")
    hidden_units = up_weight.shape[1]
    wide = HEADS * HD
    per = three.rows // panel
    plan = [(one, 0, 0, 0), (two, 0, 0, LANES)]
    plan += [(three, at * panel, 1, at * LANES) for at in range(per)]
    plan += [(four, at * panel, 1, (per + at) * LANES) for at in range(per // 2)]
    plan += [(five, at * panel, 1, (per + per // 2 + at) * LANES) for at in range(per // 2)]
    plan += [(out, 0, 2, 0), (out, panel, 2, LANES)]
    plan += [(query_one, 0, 3, 0), (query_two, 0, 3, D), (query_two, panel, 3, 2 * D)]
    plan += [(later_one, 0, 3, wide), (later_one, panel, 3, D + wide), (later_two, 0, 3, 2 * D + wide)]
    plan += [(merge_one, 0, 4, 0), (merge_two, 0, 4, LANES)]
    down_weight_grad, up_weight_grad, out_weight_grad, qkv_weight_grad, merge_weight_grad, *small = finish(
        [
            (hidden_units // devices, D),
            (D // devices, hidden_units),
            (D // devices, D),
            (D // devices, 3 * D),
            (2 * D // devices, D),
        ],
        plan,
        vectors,
        (D // devices, hidden_units // devices),
    )
    gain_one, shift_one, merge_bias_grad, gain_two, shift_two, down_bias_grad, up_bias_grad = [
        each.reshape(-1) for each in small
    ]
    return (
        output,
        frames_grad,
        skip_grad,
        merge_weight_grad,
        merge_bias_grad,
        gain_one,
        shift_one,
        qkv_weight_grad,
        out_weight_grad,
        gain_two,
        shift_two,
        up_weight_grad,
        up_bias_grad,
        down_weight_grad,
        down_bias_grad,
    )


def moved_kernel(source, target):
    target[...] = source[...]


def moved(value):
    rows = pl.BlockSpec((TILE, D), lambda i: (i, 0))
    return pl.pallas_call(
        moved_kernel,
        grid=(value.shape[0] // TILE,),
        in_specs=[rows],
        out_specs=rows,
        out_shape=jax.ShapeDtypeStruct(value.shape, value.dtype),
        compiler_params=settings(12),
        name="moved",
    )(value)


def cuts(piece, digit):
    return ((0, piece.rows, digit),)


def solution(mesh):
    rows = P(("half", "dp"), None)
    parts = P(("half", "dp"))
    in_specs = (rows, rows, rows) + (P(),) * 12 + (rows,)
    out_specs = (rows, rows, rows, rows, parts, parts, parts, rows, rows, parts, parts, rows, parts, rows, parts)
    return jax.shard_map(
        on_device, mesh=mesh, in_specs=in_specs, out_specs=out_specs, check_vma=False
    )
```
